128 devices in a mesh: seq: 8 (over y_lo, z), wide: 16 (over x, y_hi, core).
Axes of the slice: x: 4, y: 4 (y_hi: 2, y_lo: 2; y = y_hi * 2 + y_lo), z: 4, core: 2. Of those that a mesh axis runs over, the one named last changes fastest.
Arguments:
- activations: bfloat16 [8, 5120], P(None, 'wide'), may hold values from -6 to 6
- attn_gain: float32 [5120], P('wide'), may hold values from 0.25 to 1.75
- w_query: bfloat16 [5120, 8192], P('wide', 'seq'), may hold values from -0.078125 to 0.078125
- w_keyval: bfloat16 [5120, 2, 1024], P('wide', None, 'seq'), may hold values from -0.078125 to 0.078125
- w_output: bfloat16 [8192, 5120], P('seq', 'wide'), may hold values from -0.0625 to 0.0625
- query_gain: float32 [128], replicated, may hold values from 1.5 to 3
- key_gain: float32 [128], replicated, may hold values from 1.5 to 3
- key_cache: bfloat16 [8, 65536, 8, 128], P(None, ('seq', 'wide')), may hold values from -400 to 400
- value_cache: bfloat16 [8, 65536, 8, 128], P(None, ('seq', 'wide')), may hold values from -6 to 6
- lengths: int32 [8], replicated, may hold values from 8192 to 65536, as said below
Outputs:
- attended: float32 [8, 5120], P(None, 'wide')
The draws below stay inside these ranges and needn't reach their ends.
Inputs may be any that keep to these rules, and one draw needn't show every extreme that they name: `lengths`: some sequence has exactly 65536 valid positions.
All inputs are finite; a program needn't handle non-finite values.
Results may differ from the reference program's by a relative error of at most 0.014.
The reference program's roundings to bfloat16 on the way count: a program that leaves them out, or rounds other values in their place, can miss the bound.
Values may be sent and summed in bfloat16 or wider, within the bound.
A program may use at most 128 MiB of HBM per device.

```python
import math
import jax
import jax.numpy as jnp
from jax import lax

D = 5120
H = 64
KVH = 8
HD = 128
ROWS = 8
LENGTH = 65536


def draw_key_cache(key, part):
    key = jax.random.fold_in(key, 5)
    key_base = jax.random.fold_in(key, 0)
    shape = (ROWS, LENGTH, KVH, HD)
    base = jax.random.normal(key_base, shape, jnp.float32)
    base = jnp.clip(base, -6.0, 6.0)
    return base.astype(jnp.bfloat16)


def draw_lengths(key, part):
    key = jax.random.fold_in(key, 7)
    key_vals, key_top = jax.random.split(key)
    values = jax.random.randint(key_vals, (ROWS,), LENGTH // 8, LENGTH + 1)
    longest = jax.random.randint(key_top, (), 0, ROWS)
    return jnp.where(jnp.arange(ROWS) == longest, LENGTH, values).astype(jnp.int32)


def steps_of(stream_key, shape, cuts, least, top_value):
    loudness, own = 1.0, jax.random.fold_in(stream_key, 6)
    for position, blocks in cuts:
        draws = jnp.exp(jax.random.uniform(jax.random.fold_in(own, position), (blocks,), jnp.float32, least / len(cuts), top_value / len(cuts)))
        loudness = loudness * jnp.repeat(draws, shape[position] // blocks).reshape([-1 if axis == position else 1 for axis in range(len(shape))])
    return loudness


def gaussian(own_key, extent, width, limit, cuts=(), held_as=jnp.bfloat16):
    values = jax.random.normal(own_key, extent, jnp.float32) * width
    if len(cuts) > 0:
        values = steps_of(own_key, extent, cuts, -0.22, 0.18) * values
    return jnp.clip(values, min=-limit, max=limit).astype(held_as)


def setup_inputs(seed: int = 0) -> dict:
    seeds = jax.random.split(jax.random.key(seed), 11)
    return {
        "activations": gaussian(seeds[0], (ROWS, D), 1.0, 6.0, ((1, 16),)),
        "attn_gain": jnp.clip(1.0 + 0.15 * jax.random.normal(seeds[1], (D,), jnp.float32), 0.25, 1.75),
        "w_query": gaussian(seeds[2], (D, H * HD), D ** -0.5, 0.078125, ((0, 16), (1, 8))),
        "w_keyval": gaussian(seeds[3], (D, 2, KVH * HD), D ** -0.5, 0.078125, ((0, 16), (2, 8))),
        "w_output": gaussian(seeds[4], (H * HD, D), (H * HD) ** -0.5, 0.0625, ((0, 8), (1, 16))),
        "query_gain": jnp.clip(jax.random.uniform(seeds[5], (HD,), jnp.float32, 1.5, 3.0), 1.5, 3.0),
        "key_gain": jnp.clip(jax.random.uniform(seeds[6], (HD,), jnp.float32, 1.5, 3.0), 1.5, 3.0),
        "key_cache": draw_key_cache(jax.random.fold_in(seeds[10], 71), 0),
        "value_cache": gaussian(seeds[8], (ROWS, LENGTH, KVH, HD), 1.0, 6.0, ((1, 128),)),
        "lengths": draw_lengths(jax.random.fold_in(seeds[10], 71), 0),
    }


rope_base = 1000000.0
eps_norm = 1e-06

def rotate_pos(vector, positions):
    half = vector.shape[-1] // 2
    freq_index = jnp.arange(half, dtype=jnp.float32)
    inverse_freq = jnp.exp(-(2.0 * freq_index / vector.shape[-1]) * math.log(rope_base))
    angles = positions.astype(jnp.float32)[:, None, None] * inverse_freq
    cosine = jnp.cos(angles)
    sine = jnp.sin(angles)
    first_half = vector[..., :half]
    second_half = vector[..., half:]
    return jnp.concatenate([first_half * cosine - second_half * sine, second_half * cosine + first_half * sine], axis=-1)

def head_norm(vector, gain):
    return vector * lax.rsqrt(lax.optimization_barrier(jnp.mean(vector * vector, axis=-1, keepdims=True)) + eps_norm) * gain

def reference(activations, attn_gain, w_query, w_keyval, w_output, query_gain, key_gain, key_cache, value_cache, lengths):
    row_count = activations.shape[0]
    x_float = activations.astype(jnp.float32)
    inv_rms = lax.rsqrt(lax.optimization_barrier(jnp.mean(x_float * x_float, axis=-1)) + eps_norm)
    normed = (x_float * attn_gain).astype(jnp.bfloat16)
    query = jnp.dot(normed, w_query, preferred_element_type=jnp.float32) * inv_rms[:, None]
    keyval = jnp.dot(normed, w_keyval.reshape(D, 2 * KVH * HD), preferred_element_type=jnp.float32) * inv_rms[:, None]
    keyval = keyval.reshape(row_count, 2, KVH, HD)
    query_rows = rotate_pos(head_norm(query.reshape(row_count, H, HD), query_gain), lengths).astype(jnp.bfloat16)
    key_fresh = rotate_pos(head_norm(keyval[:, 0], key_gain), lengths).astype(jnp.bfloat16)
    value_fresh = keyval[:, 1].astype(jnp.bfloat16)
    group_size = H // KVH
    grouped = query_rows.reshape(row_count, KVH, group_size, HD)
    score_scale = HD ** (-0.5)
    in_cache = jnp.arange(LENGTH, dtype=jnp.int32)[None, :] < lengths[:, None]

    def one_group(kv_index):
        query_head = grouped[:, kv_index].astype(jnp.float32)
        keys_head = key_cache[:, :, kv_index].astype(jnp.float32)
        values_head = value_cache[:, :, kv_index].astype(jnp.float32)
        scores = jnp.einsum('bjd,btd->bjt', query_head, keys_head) * score_scale
        scores = jnp.where(in_cache[:, None, :], scores, -1e+30)
        fresh_score = jnp.einsum('bjd,bd->bj', query_head, key_fresh[:, kv_index].astype(jnp.float32)) * score_scale
        peak_score = jnp.maximum(lax.optimization_barrier(jnp.max(scores, axis=-1)), fresh_score)
        weights = jnp.where(in_cache[:, None, :], jnp.exp(scores - peak_score[..., None]), 0.0)
        fresh_weight = jnp.exp(fresh_score - peak_score)
        row_total = lax.optimization_barrier(jnp.sum(weights, axis=-1)) + fresh_weight
        weights_low = lax.optimization_barrier(weights.astype(jnp.bfloat16)).astype(jnp.float32)
        fresh_low = lax.optimization_barrier(fresh_weight.astype(jnp.bfloat16)).astype(jnp.float32)
        numerator = jnp.einsum('bjt,btd->bjd', weights_low, values_head)
        numerator = numerator + fresh_low[..., None] * value_fresh[:, kv_index].astype(jnp.float32)[:, None, :]
        return numerator / row_total[..., None]
    attended_heads = lax.map(one_group, jnp.arange(KVH, dtype=jnp.int32))
    attended_heads = jnp.transpose(attended_heads, (1, 0, 2, 3)).reshape(row_count, H * HD).astype(jnp.bfloat16)
    return jnp.dot(attended_heads, w_output, preferred_element_type=jnp.float32)
```

```python
import math

import jax
import jax.numpy as jnp
import numpy as np
from jax import lax
from jax.experimental import pallas as pl
from jax.experimental.pallas import tpu as pltpu
from jax.sharding import PartitionSpec as P

rope_base = 1000000.0
eps_norm = 1e-06
neg_large = -1e30
MESH = pl.DeviceIdType.MESH
f32 = jnp.float32
bf16 = jnp.bfloat16

ROWS, KVH, GROUP, HD = 8, 8, 8, 128
HEADS = KVH * GROUP
BLOCK = 512
FLAT = BLOCK * KVH
CHUNK = 512
CHUNKS = FLAT // CHUNK
NSEQ, NWIDE = 8, 16
WIDTH = 320
D = 5120


def lane_iota(shape):
    return lax.broadcasted_iota(jnp.int32, shape, len(shape) - 1)


def kernel(
    x_hbm, gain_hbm, wq_hbm, wkv_hbm, wo_hbm, qg_hbm, kg_hbm, k_hbm, v_hbm, freq_hbm, len_ref,
    out_ref,
    x_v, gain_v, wq_v, wkv_v, wo_v, qg_v, kg_v, k_v, v_v, freq_v,
    s1, r1, skv, rkv, sq, qall, qf, qt, knew, vnew, scr, mst, lst, numf,
    s3n, s3t, r3n, r3t, s4n, s4t, r4n, r4t, of, s5, r5,
    in_sem, k_sem, v_sem, ssem, rsem,
):
    s = lax.axis_index("seq")
    w = lax.axis_index("wide")
    x = w // 4
    yh = (w // 2) % 2
    core = w % 2
    yl = s // 4
    z = s % 4

    small = [
        pltpu.make_async_copy(a, b, in_sem.at[i])
        for i, (a, b) in enumerate(
            [
                (x_hbm, x_v),
                (gain_hbm, gain_v),
                (wq_hbm, wq_v),
                (qg_hbm, qg_v),
                (kg_hbm, kg_v),
                (freq_hbm, freq_v),
                (wkv_hbm, wkv_v),
                (wo_hbm, wo_v),
            ]
        )
    ]
    for c in small[:6]:
        c.start()

    wide_to = []
    for kx in (2, 1, 3, 0):
        for ky in (1, 0):
            for kc in (0, 1):
                if kx or ky or kc:
                    wide_to.append(((x + kx) % 4) * 4 + ((yh + ky) % 2) * 2 + (core + kc) % 2)
    plane_to = []
    for kz in (2, 1, 3, 0):
        for ky in (1, 0):
            for kh in (1, 0):
                for kc in (0, 1):
                    if kz or ky or kh or kc:
                        plane_to.append(
                            (
                                ((yl + ky) % 2) * 4 + (z + kz) % 4,
                                x * 4 + ((yh + kh) % 2) * 2 + (core + kc) % 2,
                                bool(kz or ky),
                            )
                        )
    seq_to = []
    for kz in (2, 1, 3, 0):
        for ky in (1, 0):
            if kz or ky:
                seq_to.append(((yl + ky) % 2) * 4 + (z + kz) % 4)

    bar = pltpu.get_barrier_semaphore()
    n_bar = 0
    for tw in wide_to:
        pl.semaphore_signal(bar, inc=1, device_id=(s, tw), device_id_type=MESH)
        n_bar += 1
    for ts, tw, far in plane_to:
        if far:
            pl.semaphore_signal(bar, inc=1, device_id=(ts, tw), device_id_type=MESH)
            n_bar += 1

    for c in small[6:]:
        c.start()
    k_cp = [pltpu.make_async_copy(k_hbm.at[b], k_v.at[b], k_sem.at[b]) for b in range(ROWS)]
    v_cp = [pltpu.make_async_copy(v_hbm.at[b], v_v.at[b], v_sem.at[b]) for b in range(ROWS)]
    for c in k_cp + v_cp:
        c.start()

    def remote(src, dst, i, to):
        return pltpu.make_async_remote_copy(
            src_ref=src, dst_ref=dst, send_sem=ssem.at[i], recv_sem=rsem.at[i],
            device_id=to, device_id_type=MESH,
        )

    for c in small[:6]:
        c.wait()
    xf = x_v[...].astype(f32)
    ss = jnp.sum(xf * xf, axis=-1, keepdims=True)
    normed = (xf * gain_v[...][None, :]).astype(bf16)
    for p in range(4):
        part = jnp.dot(normed, wq_v[:, p * 256 : (p + 1) * 256], preferred_element_type=f32)
        s1[p, 0] = part[:, :HD]
        s1[p, 1] = part[:, HD:]
        s1[p, 2] = jnp.broadcast_to(ss, (ROWS, HD))
    r1[w] = s1[w % 4]

    pl.semaphore_wait(bar, n_bar)
    for tw in wide_to:
        remote(s1.at[tw % 4], r1.at[w], 0, (s, tw)).start()

    small[6].wait()
    row_i = lax.broadcasted_iota(jnp.int32, (WIDTH, 2 * WIDTH), 0)
    col_i = lax.broadcasted_iota(jnp.int32, (WIDTH, 2 * WIDTH), 1)
    spread = jnp.where(col_i // 2 == row_i, 1.0, 0.0).astype(bf16)
    twice = jnp.dot(normed, spread, preferred_element_type=f32)
    odd = lane_iota((ROWS, 2 * WIDTH)) % 2
    both = jnp.concatenate(
        [jnp.where(odd == 0, twice, 0.0), jnp.where(odd == 1, twice, 0.0)], axis=0
    ).astype(bf16)
    kv_part = jnp.dot(both, wkv_v[...], preferred_element_type=f32)
    skv[0] = kv_part[:ROWS]
    skv[1] = kv_part[ROWS:]
    for t in range(2):

        @pl.when(w != t)
        def _():
            remote(skv, rkv.at[w], 1, (s, t)).start()

        @pl.when(w == t)
        def _():
            rkv[w] = skv[...]

    row = lax.broadcasted_iota(jnp.int32, (ROWS, HD), 0)
    lane = lane_iota((ROWS, HD))
    lens = jnp.zeros((ROWS, HD), jnp.int32)
    for b in range(ROWS):
        lens = jnp.where(row == b, len_ref[b], lens)
    angle = lens.astype(f32) * freq_v[...]
    cosine = jnp.cos(angle)
    sine = jnp.where(lane < HD // 2, -jnp.sin(angle), jnp.sin(angle))

    def head(u, gain):
        u = u * lax.rsqrt(jnp.mean(u * u, axis=-1, keepdims=True) + eps_norm) * gain
        return u * cosine + pltpu.roll(u, HD // 2, 1) * sine

    remote(r1.at[pl.ds(0, NWIDE - 1)], r1.at[pl.ds(0, NWIDE - 1)], 0, (s, w)).wait_recv()
    tot = r1[0]
    for i in range(1, NWIDE):
        tot = tot + r1[i]
    inv_rms = lax.rsqrt(tot[2] / D + eps_norm)
    sq[...] = jnp.concatenate(
        [head(tot[0] * inv_rms, qg_v[...]), head(tot[1] * inv_rms, qg_v[...])], axis=0
    ).astype(bf16)

    p_own = w % 4
    for ts, tw, _far in plane_to:
        remote(sq, qall.at[s * 4 + p_own], 2, (ts, tw)).start()
    qall[s * 4 + p_own] = sq[...]

    @pl.when(w < 2)
    def _():
        remote(rkv.at[pl.ds(0, NWIDE - 1)], rkv.at[pl.ds(0, NWIDE - 1)], 1, (s, w)).wait_recv()
        kv = rkv[0]
        for i in range(1, NWIDE):
            kv = kv + rkv[i]
        knew[...] = head(kv[0] * inv_rms, kg_v[...]).astype(bf16).astype(f32)
        vnew[...] = (kv[1] * inv_rms).astype(bf16).astype(f32)

    remote(qall.at[pl.ds(0, 31)], qall.at[pl.ds(0, 31)], 2, (s, w)).wait_recv()
    qf[...] = qall[...].reshape(HEADS * ROWS, HD).astype(f32)
    for b in range(ROWS):
        qt[b] = qf[pl.ds(b, HEADS, stride=ROWS), :]

    scale = HD ** (-0.5)
    start = (s * NWIDE + w) * BLOCK
    clane = lane_iota((GROUP, CHUNK))
    bit0 = clane % 2 == 1
    bit1 = (clane // 2) % 2 == 1
    bit2 = (clane // 4) % 2 == 1
    of_group = [clane % KVH == g for g in range(KVH)]

    def attend(b, carry):
        q = qt[b].astype(bf16)
        limit = (len_ref[b] - start) * KVH
        peak = jnp.full((GROUP, CHUNK), neg_large, f32)
        for ch in range(CHUNKS):
            keys = k_v[b, pl.ds(ch * CHUNK, CHUNK), :]
            sc = lax.dot_general(q, keys, (((1,), (1,)), ((), ())), preferred_element_type=f32)
            g = [sc[i * GROUP : (i + 1) * GROUP] for i in range(KVH)]
            g = [jnp.where(bit0, g[i + 1], g[i]) for i in range(0, 8, 2)]
            g = [jnp.where(bit1, g[i + 1], g[i]) for i in range(0, 4, 2)]
            t = jnp.where(bit2, g[1], g[0]) * scale
            t = jnp.where(clane + ch * CHUNK < limit, t, neg_large)
            scr[ch] = t
            peak = jnp.maximum(peak, t)
        m = jnp.maximum(
            jnp.maximum(peak[:, 0:128], peak[:, 128:256]),
            jnp.maximum(peak[:, 256:384], peak[:, 384:512]),
        )
        for sh in (64, 32, 16, 8):
            m = jnp.maximum(m, pltpu.roll(m, sh, 1))
        m4 = jnp.concatenate([m, m, m, m], axis=1)
        total = jnp.zeros((GROUP, CHUNK), f32)
        num = jnp.zeros((HEADS, HD), f32)
        for ch in range(CHUNKS):
            e = jnp.exp(scr[ch] - m4)
            e = jnp.where(clane + ch * CHUNK < limit, e, 0.0)
            total = total + e
            wide_e = jnp.concatenate(
                [jnp.where(of_group[g], e, 0.0) for g in range(KVH)], axis=0
            ).astype(bf16)
            num = num + jnp.dot(
                wide_e, v_v[b, pl.ds(ch * CHUNK, CHUNK), :], preferred_element_type=f32
            )
        tl = total[:, 0:128] + total[:, 128:256] + total[:, 256:384] + total[:, 384:512]
        for sh in (64, 32, 16, 8):
            tl = tl + pltpu.roll(tl, sh, 1)
        mst[b] = m
        lst[b] = tl
        numf[b] = num.reshape(KVH, GROUP, HD)
        return carry

    block32 = lane // 32
    low16 = lane % 32 < 16

    def by_block(parts):
        out = parts[0]
        for i in range(1, 4):
            out = jnp.where(block32 == i, parts[i], out)
        return out

    slot3 = s * 2 + core
    for c in range(2):
        for b in range(c * 4, c * 4 + 4):
            k_cp[b].wait()
            v_cp[b].wait()
        lax.fori_loop(c * 4, c * 4 + 4, attend, 0)
        s3t[c] = jnp.where(
            low16,
            by_block([mst[c * 4 + i] for i in range(4)]),
            by_block([lst[c * 4 + i] for i in range(4)]),
        )
        for g in range(KVH):
            s3n[c, g] = jnp.concatenate([numf[c * 4 + i, g] for i in range(4)], axis=0).astype(bf16)
        tw = w - core + c
        for ts in seq_to:
            remote(s3n.at[c, ts], r3n.at[slot3], 3, (ts, tw)).start()
            remote(s3t.at[c], r3t.at[slot3], 4, (ts, tw)).start()

        @pl.when(core != c)
        def _():
            remote(s3n.at[c, s], r3n.at[slot3], 3, (s, tw)).start()
            remote(s3t.at[c], r3t.at[slot3], 4, (s, tw)).start()

        @pl.when(core == c)
        def _():
            r3n[slot3] = s3n[c, s]
            r3t[slot3] = s3t[c]

    @pl.when(w < 2)
    def _():
        parts = []
        for i in range(4):
            b = core * 4 + i
            qrow = qt[b, pl.ds(s * GROUP, GROUP), :]
            sn = jnp.sum(qrow * knew[pl.ds(b, 1), :], axis=-1, keepdims=True) * scale
            parts.append(jnp.broadcast_to(sn, (GROUP, HD)))
        r3t[16] = jnp.where(low16, by_block(parts), 1.0)
        r3n[16] = jnp.concatenate(
            [jnp.broadcast_to(vnew[pl.ds(core * 4 + i, 1), :], (GROUP, HD)) for i in range(4)], axis=0
        ).astype(bf16)

    @pl.when(w >= 2)
    def _():
        r3t[16] = jnp.where(low16, neg_large, 0.0)
        r3n[16] = jnp.zeros((32, HD), bf16)

    remote(r3t.at[pl.ds(0, 15)], r3t.at[pl.ds(0, 15)], 4, (s, w)).wait_recv()
    remote(r3n.at[pl.ds(0, 15)], r3n.at[pl.ds(0, 15)], 3, (s, w)).wait_recv()

    def merge(stats, numers):
        peak = stats[0]
        for t in stats[1:]:
            peak = jnp.maximum(peak, t)
        total = jnp.zeros((GROUP, HD), f32)
        acc = [jnp.zeros((GROUP, HD), f32) for _ in range(4)]
        for t, n in zip(stats, numers):
            f = jnp.exp(t - peak)
            total = total + f * pltpu.roll(t, HD - 16, 1)
            for i in range(4):
                acc[i] = acc[i] + jnp.broadcast_to(f[:, 32 * i : 32 * i + 1], (GROUP, HD)) * n[
                    i * GROUP : (i + 1) * GROUP
                ]
        return peak, total, acc

    shift = (HD - s) % HD
    peak, total, acc = merge(
        [pltpu.roll(r3t[i], shift, 1) for i in range(17)],
        [r3n[i].astype(f32) for i in range(17)],
    )
    s4t[...] = jnp.where(low16, peak, pltpu.roll(total, 16, 1))
    s4n[...] = jnp.concatenate(acc, axis=0).astype(bf16)
    for tw in wide_to:
        remote(s4n, r4n.at[w], 5, (s, tw)).start()
        remote(s4t, r4t.at[w], 6, (s, tw)).start()
    r4n[w] = s4n[...]
    r4t[w] = s4t[...]
    small[7].wait()
    remote(r4t.at[pl.ds(0, 15)], r4t.at[pl.ds(0, 15)], 6, (s, w)).wait_recv()
    remote(r4n.at[pl.ds(0, 15)], r4n.at[pl.ds(0, 15)], 5, (s, w)).wait_recv()
    for c in range(2):
        peak, total, acc = merge(
            [r4t[2 * i + c] for i in range(8)], [r4n[2 * i + c].astype(f32) for i in range(8)]
        )
        for i in range(4):
            den = jnp.broadcast_to(total[:, 32 * i : 32 * i + 1], (GROUP, HD))
            of[pl.ds((c * 4 + i) * GROUP, GROUP), :] = acc[i] / den

    o = jnp.concatenate(
        [of[pl.ds(j, ROWS, stride=GROUP), :].astype(bf16) for j in range(GROUP)], axis=1
    )
    s5[...] = lax.dot_general(o, wo_v[...], (((1,), (1,)), ((), ())), preferred_element_type=f32)
    for ts in seq_to:
        remote(s5, r5.at[s], 7, (ts, w)).start()
    r5[s] = s5[...]
    remote(r5.at[pl.ds(0, 7)], r5.at[pl.ds(0, 7)], 7, (s, w)).wait_recv()
    out = r5[0]
    for i in range(1, NSEQ):
        out = out + r5[i]
    out_ref[...] = out

    remote(r1.at[pl.ds(0, 15)], r1.at[pl.ds(0, 15)], 0, (s, w)).wait_send()
    for t in range(2):

        @pl.when(w != t)
        def _():
            remote(skv, rkv.at[w], 1, (s, t)).wait_send()

    remote(qall.at[pl.ds(0, 31)], qall.at[pl.ds(0, 31)], 2, (s, w)).wait_send()
    remote(r3n.at[pl.ds(0, 15)], r3n.at[pl.ds(0, 15)], 3, (s, w)).wait_send()
    remote(r3t.at[pl.ds(0, 15)], r3t.at[pl.ds(0, 15)], 4, (s, w)).wait_send()
    remote(r4n.at[pl.ds(0, 15)], r4n.at[pl.ds(0, 15)], 5, (s, w)).wait_send()
    remote(r4t.at[pl.ds(0, 15)], r4t.at[pl.ds(0, 15)], 6, (s, w)).wait_send()
    remote(r5.at[pl.ds(0, 7)], r5.at[pl.ds(0, 7)], 7, (s, w)).wait_send()


def body(
    activations, attn_gain, w_query, w_keyval, w_output, query_gain, key_gain, key_cache, value_cache, lengths
):
    half = HD // 2
    freq = np.exp(-(2.0 * np.arange(half) / HD) * math.log(rope_base)).astype(np.float32)
    freq = jnp.asarray(np.concatenate([freq, freq])[None, :])
    any_spec = pl.BlockSpec(memory_space=pl.ANY)
    vm = pltpu.VMEM
    return pl.pallas_call(
        kernel,
        out_shape=jax.ShapeDtypeStruct((ROWS, WIDTH), f32),
        in_specs=[any_spec] * 10 + [pl.BlockSpec(memory_space=pltpu.SMEM)],
        out_specs=pl.BlockSpec(memory_space=pltpu.VMEM),
        scratch_shapes=[
            vm((ROWS, WIDTH), bf16),
            vm((WIDTH,), f32),
            vm((WIDTH, 1024), bf16),
            vm((2 * WIDTH, HD), bf16),
            vm((WIDTH, 1024), bf16),
            vm((1, HD), f32),
            vm((1, HD), f32),
            vm((ROWS, FLAT, HD), bf16),
            vm((ROWS, FLAT, HD), bf16),
            vm((1, HD), f32),
            vm((4, 3, ROWS, HD), f32),
            vm((NWIDE, 3, ROWS, HD), f32),
            vm((2, ROWS, HD), f32),
            vm((NWIDE, 2, ROWS, HD), f32),
            vm((16, HD), bf16),
            vm((32, 16, HD), bf16),
            vm((HEADS * ROWS, HD), f32),
            vm((ROWS, HEADS, HD), f32),
            vm((ROWS, HD), f32),
            vm((ROWS, HD), f32),
            vm((CHUNKS, GROUP, CHUNK), f32),
            vm((ROWS, GROUP, HD), f32),
            vm((ROWS, GROUP, HD), f32),
            vm((ROWS, KVH, GROUP, HD), f32),
            vm((2, KVH, 32, HD), bf16),
            vm((2, GROUP, HD), f32),
            vm((17, 32, HD), bf16),
            vm((17, GROUP, HD), f32),
            vm((32, HD), bf16),
            vm((GROUP, HD), f32),
            vm((NWIDE, 32, HD), bf16),
            vm((NWIDE, GROUP, HD), f32),
            vm((HEADS, HD), f32),
            vm((ROWS, WIDTH), f32),
            vm((NSEQ, ROWS, WIDTH), f32),
            pltpu.SemaphoreType.DMA((8,)),
            pltpu.SemaphoreType.DMA((ROWS,)),
            pltpu.SemaphoreType.DMA((ROWS,)),
            pltpu.SemaphoreType.DMA((8,)),
            pltpu.SemaphoreType.DMA((8,)),
        ],
        compiler_params=pltpu.CompilerParams(
            collective_id=0, has_side_effects=True, vmem_limit_bytes=60 * 1024 * 1024
        ),
    )(
        activations,
        attn_gain,
        w_query,
        w_keyval.reshape(2 * WIDTH, HD),
        w_output.T,
        query_gain.reshape(1, HD),
        key_gain.reshape(1, HD),
        key_cache.reshape(ROWS, FLAT, HD),
        value_cache.reshape(ROWS, FLAT, HD),
        freq,
        lengths,
    )


def solution(mesh):
    return jax.shard_map(
        body,
        mesh=mesh,
        in_specs=(
            P(None, "wide"),
            P("wide"),
            P("wide", "seq"),
            P("wide", None, "seq"),
            P("seq", "wide"),
            P(),
            P(),
            P(None, ("seq", "wide"), None, None),
            P(None, ("seq", "wide"), None, None),
            P(),
        ),
        out_specs=P(None, "wide"),
        check_vma=False,
    )
```

```python
import math

import jax
import jax.numpy as jnp
import numpy as np
from jax import lax
from jax.experimental import pallas as pl
from jax.experimental.pallas import tpu as pltpu
from jax.sharding import PartitionSpec as P

rope_base = 1000000.0
eps_norm = 1e-06
neg_large = -1e30
MESH = pl.DeviceIdType.MESH
f32 = jnp.float32
bf16 = jnp.bfloat16

ROWS, KVH, GROUP, HD = 8, 8, 8, 128
HEADS = KVH * GROUP
BLOCK = 512
FLAT = BLOCK * KVH
NSEQ, NWIDE = 8, 16
WIDTH = 320
D = 5120


def lane_iota(shape):
    return lax.broadcasted_iota(jnp.int32, shape, len(shape) - 1)


def kernel(
    x_hbm, gain_hbm, wq_hbm, wkv_hbm, wo_hbm, qg_hbm, kg_hbm, k_hbm, v_hbm, freq_hbm, len_ref,
    out_ref,
    x_v, gain_v, wq_v, wkv_v, wo_v, qg_v, kg_v, k_v, v_v, freq_v,
    k_t, v_r, s1, r1, skv, rkv, sq, qall, qf, qt, knew, vnew, scr, pb,
    s3n, s3t, r3n, r3t, s4n, s4t, r4n, r4t, of, s5, r5,
    in_sem, k_sem, v_sem, ssem, rsem,
):
    s = lax.axis_index("seq")
    w = lax.axis_index("wide")
    x = w // 4
    yh = (w // 2) % 2
    core = w % 2
    yl = s // 4
    z = s % 4

    small = [
        pltpu.make_async_copy(a, b, in_sem.at[i])
        for i, (a, b) in enumerate(
            [
                (x_hbm, x_v),
                (gain_hbm, gain_v),
                (wq_hbm, wq_v),
                (qg_hbm, qg_v),
                (kg_hbm, kg_v),
                (freq_hbm, freq_v),
                (wkv_hbm, wkv_v),
                (wo_hbm, wo_v),
            ]
        )
    ]
    for c in small[:6]:
        c.start()

    wide_to = []
    for kx in (2, 1, 3, 0):
        for ky in (1, 0):
            for kc in (0, 1):
                if kx or ky or kc:
                    wide_to.append(((x + kx) % 4) * 4 + ((yh + ky) % 2) * 2 + (core + kc) % 2)
    plane_to = []
    for kz in (2, 1, 3, 0):
        for ky in (1, 0):
            for kh in (1, 0):
                for kc in (0, 1):
                    if kz or ky or kh or kc:
                        plane_to.append(
                            (
                                ((yl + ky) % 2) * 4 + (z + kz) % 4,
                                x * 4 + ((yh + kh) % 2) * 2 + (core + kc) % 2,
                                bool(kz or ky),
                            )
                        )
    seq_to = []
    for kz in (2, 1, 3, 0):
        for ky in (1, 0):
            if kz or ky:
                seq_to.append(((yl + ky) % 2) * 4 + (z + kz) % 4)

    bar = pltpu.get_barrier_semaphore()
    n_bar = 0
    for tw in wide_to:
        pl.semaphore_signal(bar, inc=1, device_id=(s, tw), device_id_type=MESH)
        n_bar += 1
    for ts, tw, far in plane_to:
        if far:
            pl.semaphore_signal(bar, inc=1, device_id=(ts, tw), device_id_type=MESH)
            n_bar += 1

    for c in small[6:]:
        c.start()
    k_cp = [pltpu.make_async_copy(k_hbm.at[b], k_v.at[b], k_sem.at[b]) for b in range(ROWS)]
    v_cp = [pltpu.make_async_copy(v_hbm.at[b], v_v.at[b], v_sem.at[b]) for b in range(ROWS)]
    for c in k_cp + v_cp:
        c.start()

    def remote(src, dst, i, to):
        return pltpu.make_async_remote_copy(
            src_ref=src, dst_ref=dst, send_sem=ssem.at[i], recv_sem=rsem.at[i],
            device_id=to, device_id_type=MESH,
        )

    for c in small[:6]:
        c.wait()
    xf = x_v[...].astype(f32)
    ss = jnp.sum(xf * xf, axis=-1, keepdims=True)
    normed = (xf * gain_v[...][None, :]).astype(bf16)
    row = lax.broadcasted_iota(jnp.int32, (ROWS, HD), 0)
    lane = lane_iota((ROWS, HD))
    ss_row = jnp.sum(jnp.where(lane == row, ss, 0.0), axis=0, keepdims=True)
    for p in range(4):
        part = jnp.dot(normed, wq_v[:, p * 256 : (p + 1) * 256], preferred_element_type=f32)
        s1[p, 0:ROWS] = part[:, :HD]
        s1[p, ROWS : 2 * ROWS] = part[:, HD:]
        s1[p, 2 * ROWS : 2 * ROWS + 1] = ss_row
    r1[w] = s1[w % 4]

    def turn_k(b, carry):
        pltpu.make_async_copy(k_hbm.at[b], k_v.at[b], k_sem.at[b]).wait()
        for ch in range(2):
            part = k_v[b, pl.ds(ch * 2048, 2048), :].reshape(256, KVH, HD).reshape(256, KVH * HD)
            k_t[b, :, ch * 256 : (ch + 1) * 256] = part.T
        return carry

    def turn_v(b, carry):
        pltpu.make_async_copy(v_hbm.at[b], v_v.at[b], v_sem.at[b]).wait()
        for ch in range(2):
            part = v_v[b, pl.ds(ch * 2048, 2048), :].reshape(256, KVH, HD)
            v_r[b, pl.ds(ch * 256, 256), :] = part.reshape(256, KVH * HD)
        return carry

    pl.semaphore_wait(bar, n_bar)
    for tw in wide_to:
        remote(s1.at[tw % 4], r1.at[w], 0, (s, tw)).start()

    small[6].wait()
    row_i = lax.broadcasted_iota(jnp.int32, (WIDTH, 2 * WIDTH), 0)
    col_i = lax.broadcasted_iota(jnp.int32, (WIDTH, 2 * WIDTH), 1)
    spread = jnp.where(col_i // 2 == row_i, 1.0, 0.0).astype(bf16)
    twice = jnp.dot(normed, spread, preferred_element_type=f32)
    odd = lane_iota((ROWS, 2 * WIDTH)) % 2
    both = jnp.concatenate(
        [jnp.where(odd == 0, twice, 0.0), jnp.where(odd == 1, twice, 0.0)], axis=0
    ).astype(bf16)
    kv_part = jnp.dot(both, wkv_v[...], preferred_element_type=f32)
    skv[0] = kv_part[:ROWS]
    skv[1] = kv_part[ROWS:]

    lens = jnp.zeros((ROWS, HD), jnp.int32)
    for b in range(ROWS):
        lens = jnp.where(row == b, len_ref[b], lens)
    angle = lens.astype(f32) * freq_v[...]
    cosine = jnp.cos(angle)
    sine = jnp.where(lane < HD // 2, -jnp.sin(angle), jnp.sin(angle))

    def head(u, gain):
        u = u * lax.rsqrt(jnp.mean(u * u, axis=-1, keepdims=True) + eps_norm) * gain
        return u * cosine + pltpu.roll(u, HD // 2, 1) * sine

    for t in range(2):

        @pl.when(w != t)
        def _():
            remote(skv, rkv.at[w], 1, (s, t)).start()

        @pl.when(w == t)
        def _():
            rkv[w] = skv[...]

    lax.fori_loop(0, 4, turn_k, 0)

    remote(r1.at[pl.ds(0, NWIDE - 1)], r1.at[pl.ds(0, NWIDE - 1)], 0, (s, w)).wait_recv()
    tot = r1[0]
    for i in range(1, NWIDE):
        tot = tot + r1[i]
    ss = jnp.sum(
        jnp.where(lane == row, tot[2 * ROWS : 2 * ROWS + 1], 0.0), axis=-1, keepdims=True
    )
    inv_rms = lax.rsqrt(ss / D + eps_norm)
    sq[...] = jnp.concatenate(
        [head(tot[:ROWS] * inv_rms, qg_v[...]), head(tot[ROWS : 2 * ROWS] * inv_rms, qg_v[...])], axis=0
    ).astype(bf16)

    p_own = w % 4
    for ts, tw, _far in plane_to:
        remote(sq, qall.at[s * 4 + p_own], 2, (ts, tw)).start()
    qall[s * 4 + p_own] = sq[...]

    @pl.when(w < 2)
    def _():
        remote(rkv.at[pl.ds(0, NWIDE - 1)], rkv.at[pl.ds(0, NWIDE - 1)], 1, (s, w)).wait_recv()
        kv = rkv[0]
        for i in range(1, NWIDE):
            kv = kv + rkv[i]
        knew[...] = head(kv[0] * inv_rms, kg_v[...]).astype(bf16).astype(f32)
        vnew[...] = (kv[1] * inv_rms).astype(bf16).astype(f32)

    lax.fori_loop(4, ROWS, turn_k, 0)
    lax.fori_loop(0, ROWS, turn_v, 0)

    remote(qall.at[pl.ds(0, 31)], qall.at[pl.ds(0, 31)], 2, (s, w)).wait_recv()
    qf[...] = qall[...].reshape(HEADS * ROWS, HD).astype(f32)
    for b in range(ROWS):
        qt[b] = qf[pl.ds(b, HEADS, stride=ROWS), :]

    scale = HD ** (-0.5)
    start = (s * NWIDE + w) * BLOCK
    plane = lane_iota((HEADS, BLOCK))
    none = jnp.zeros((GROUP, HD), f32)
    block32 = lane_iota((HEADS, HD)) // 32
    low = lane_iota((HEADS, HD)) % 32 < 16
    low16 = lane % 32 < 16

    def by_block(parts):
        n = parts[0].shape[0]
        out = parts[0]
        for i in range(1, 4):
            out = jnp.where(block32[:n] == i, parts[i], out)
        return out

    slot3 = s * 2 + core
    for c in range(2):
        rows = range(c * 4, c * 4 + 4)
        scores, peaks, totals, weights, numers = {}, {}, {}, {}, {}
        for b in rows:
            parts = []
            for pr in range(4):
                one = qt[b, 16 * pr : 16 * pr + 8, :]
                two = qt[b, 16 * pr + 8 : 16 * pr + 16, :]
                lhs = jnp.concatenate(
                    [jnp.concatenate([one, none], axis=1), jnp.concatenate([none, two], axis=1)],
                    axis=0,
                ).astype(bf16)
                keys = k_t[b, pr * 256 : (pr + 1) * 256, :]
                parts.append(jnp.dot(lhs, keys, preferred_element_type=f32))
            scr[b % 4] = jnp.concatenate(parts, axis=0)
        for b in rows:
            valid = plane < len_ref[b] - start
            t = jnp.where(valid, scr[b % 4] * scale, neg_large)
            m = jnp.max(t, axis=-1, keepdims=True)
            e = jnp.where(valid, jnp.exp(t - m), 0.0)
            peaks[b] = jnp.broadcast_to(m, (HEADS, HD))
            totals[b] = jnp.broadcast_to(jnp.sum(e, axis=-1, keepdims=True), (HEADS, HD))
            pb[b % 4] = e.astype(bf16)
        for b in rows:
            for pr in range(4):
                n = jnp.dot(
                    pb[b % 4, 16 * pr : 16 * pr + 16, :],
                    v_r[b, :, pr * 256 : (pr + 1) * 256],
                    preferred_element_type=f32,
                )
                numers[b, 2 * pr] = n[:GROUP, :HD]
                numers[b, 2 * pr + 1] = n[GROUP:, HD:]
        s3t[c] = jnp.where(
            low, by_block([peaks[b] for b in rows]), by_block([totals[b] for b in rows])
        ).reshape(KVH, GROUP, HD)
        for g in range(KVH):
            s3n[c, g] = jnp.concatenate([numers[b, g] for b in rows], axis=0).astype(bf16)
        tw = w - core + c
        for ts in seq_to:
            remote(s3n.at[c, ts], r3n.at[slot3], 3, (ts, tw)).start()
            remote(s3t.at[c, ts], r3t.at[slot3], 4, (ts, tw)).start()

        @pl.when(core != c)
        def _():
            remote(s3n.at[c, s], r3n.at[slot3], 3, (s, tw)).start()
            remote(s3t.at[c, s], r3t.at[slot3], 4, (s, tw)).start()

        @pl.when(core == c)
        def _():
            r3n[slot3] = s3n[c, s]
            r3t[slot3] = s3t[c, s]

    @pl.when(w < 2)
    def _():
        parts = []
        for i in range(4):
            b = core * 4 + i
            qrow = qt[b, pl.ds(s * GROUP, GROUP), :]
            sn = jnp.sum(qrow * knew[pl.ds(b, 1), :], axis=-1, keepdims=True) * scale
            parts.append(jnp.broadcast_to(sn, (GROUP, HD)))
        r3t[16] = jnp.where(low16, by_block(parts), 1.0)
        r3n[16] = jnp.concatenate(
            [jnp.broadcast_to(vnew[pl.ds(core * 4 + i, 1), :], (GROUP, HD)) for i in range(4)], axis=0
        ).astype(bf16)

    @pl.when(w >= 2)
    def _():
        r3t[16] = jnp.where(low16, neg_large, 0.0)
        r3n[16] = jnp.zeros((32, HD), bf16)

    remote(r3t.at[pl.ds(0, 15)], r3t.at[pl.ds(0, 15)], 4, (s, w)).wait_recv()
    remote(r3n.at[pl.ds(0, 15)], r3n.at[pl.ds(0, 15)], 3, (s, w)).wait_recv()

    def merge(stats, numers):
        peak = stats[0]
        for t in stats[1:]:
            peak = jnp.maximum(peak, t)
        total = jnp.zeros((GROUP, HD), f32)
        acc = [jnp.zeros((GROUP, HD), f32) for _ in range(4)]
        for t, n in zip(stats, numers):
            f = jnp.exp(t - peak)
            total = total + f * pltpu.roll(t, HD - 16, 1)
            for i in range(4):
                acc[i] = acc[i] + jnp.broadcast_to(f[:, 32 * i : 32 * i + 1], (GROUP, HD)) * n[
                    i * GROUP : (i + 1) * GROUP
                ]
        return peak, total, acc

    peak, total, acc = merge(
        [r3t[i] for i in range(17)],
        [r3n[i].astype(f32) for i in range(17)],
    )
    s4t[...] = jnp.where(low16, peak, pltpu.roll(total, 16, 1))
    s4n[...] = jnp.concatenate(acc, axis=0).astype(bf16)
    for tw in wide_to:
        remote(s4n, r4n.at[w], 5, (s, tw)).start()
        remote(s4t, r4t.at[w], 6, (s, tw)).start()
    r4n[w] = s4n[...]
    r4t[w] = s4t[...]
    small[7].wait()
    remote(r4t.at[pl.ds(0, 15)], r4t.at[pl.ds(0, 15)], 6, (s, w)).wait_recv()
    remote(r4n.at[pl.ds(0, 15)], r4n.at[pl.ds(0, 15)], 5, (s, w)).wait_recv()
    for c in range(2):
        peak, total, acc = merge(
            [r4t[2 * i + c] for i in range(8)], [r4n[2 * i + c].astype(f32) for i in range(8)]
        )
        for i in range(4):
            den = jnp.broadcast_to(total[:, 32 * i : 32 * i + 1], (GROUP, HD))
            of[pl.ds((c * 4 + i) * GROUP, GROUP), :] = acc[i] / den

    o = jnp.concatenate(
        [of[pl.ds(j, ROWS, stride=GROUP), :].astype(bf16) for j in range(GROUP)], axis=1
    )
    s5[...] = lax.dot_general(o, wo_v[...], (((1,), (1,)), ((), ())), preferred_element_type=f32)
    for ts in seq_to:
        remote(s5, r5.at[s], 7, (ts, w)).start()
    r5[s] = s5[...]
    remote(r5.at[pl.ds(0, 7)], r5.at[pl.ds(0, 7)], 7, (s, w)).wait_recv()
    out = r5[0]
    for i in range(1, NSEQ):
        out = out + r5[i]
    out_ref[...] = out

    remote(r1.at[pl.ds(0, 15)], r1.at[pl.ds(0, 15)], 0, (s, w)).wait_send()
    for t in range(2):

        @pl.when(w != t)
        def _():
            remote(skv, rkv.at[w], 1, (s, t)).wait_send()

    remote(qall.at[pl.ds(0, 31)], qall.at[pl.ds(0, 31)], 2, (s, w)).wait_send()
    remote(r3n.at[pl.ds(0, 15)], r3n.at[pl.ds(0, 15)], 3, (s, w)).wait_send()
    remote(r3t.at[pl.ds(0, 15)], r3t.at[pl.ds(0, 15)], 4, (s, w)).wait_send()
    remote(r4n.at[pl.ds(0, 15)], r4n.at[pl.ds(0, 15)], 5, (s, w)).wait_send()
    remote(r4t.at[pl.ds(0, 15)], r4t.at[pl.ds(0, 15)], 6, (s, w)).wait_send()
    remote(r5.at[pl.ds(0, 7)], r5.at[pl.ds(0, 7)], 7, (s, w)).wait_send()


def body(
    activations, attn_gain, w_query, w_keyval, w_output, query_gain, key_gain, key_cache, value_cache, lengths
):
    half = HD // 2
    freq = np.exp(-(2.0 * np.arange(half) / HD) * math.log(rope_base)).astype(np.float32)
    freq = jnp.asarray(np.concatenate([freq, freq])[None, :])
    any_spec = pl.BlockSpec(memory_space=pl.ANY)
    vm = pltpu.VMEM
    return pl.pallas_call(
        kernel,
        out_shape=pltpu.VMEM((ROWS, WIDTH), f32),
        in_specs=[any_spec] * 10 + [pl.BlockSpec(memory_space=pltpu.SMEM)],
        out_specs=pl.BlockSpec(memory_space=pltpu.VMEM),
        scratch_shapes=[
            vm((ROWS, WIDTH), bf16),
            vm((WIDTH,), f32),
            vm((WIDTH, 1024), bf16),
            vm((2 * WIDTH, HD), bf16),
            vm((WIDTH, 1024), bf16),
            vm((1, HD), f32),
            vm((1, HD), f32),
            vm((ROWS, FLAT, HD), bf16),
            vm((ROWS, FLAT, HD), bf16),
            vm((1, HD), f32),
            vm((ROWS, KVH * HD, BLOCK), bf16),
            vm((ROWS, BLOCK, KVH * HD), bf16),
            vm((4, 17, HD), f32),
            vm((NWIDE, 17, HD), f32),
            vm((2, ROWS, HD), f32),
            vm((NWIDE, 2, ROWS, HD), f32),
            vm((16, HD), bf16),
            vm((32, 16, HD), bf16),
            vm((HEADS * ROWS, HD), f32),
            vm((ROWS, HEADS, HD), f32),
            vm((ROWS, HD), f32),
            vm((ROWS, HD), f32),
            vm((4, HEADS, BLOCK), f32),
            vm((4, HEADS, BLOCK), bf16),
            vm((2, KVH, 32, HD), bf16),
            vm((2, KVH, GROUP, HD), f32),
            vm((17, 32, HD), bf16),
            vm((17, GROUP, HD), f32),
            vm((32, HD), bf16),
            vm((GROUP, HD), f32),
            vm((NWIDE, 32, HD), bf16),
            vm((NWIDE, GROUP, HD), f32),
            vm((HEADS, HD), f32),
            vm((ROWS, WIDTH), f32),
            vm((NSEQ, ROWS, WIDTH), f32),
            pltpu.SemaphoreType.DMA((8,)),
            pltpu.SemaphoreType.DMA((ROWS,)),
            pltpu.SemaphoreType.DMA((ROWS,)),
            pltpu.SemaphoreType.DMA((8,)),
            pltpu.SemaphoreType.DMA((8,)),
        ],
        compiler_params=pltpu.CompilerParams(
            collective_id=0, has_side_effects=True, vmem_limit_bytes=60 * 1024 * 1024
        ),
    )(
        activations,
        attn_gain,
        w_query,
        w_keyval.reshape(2 * WIDTH, HD),
        w_output.T,
        query_gain.reshape(1, HD),
        key_gain.reshape(1, HD),
        key_cache.reshape(ROWS, FLAT, HD),
        value_cache.reshape(ROWS, FLAT, HD),
        freq,
        lengths,
    )


def solution(mesh):
    return jax.shard_map(
        body,
        mesh=mesh,
        in_specs=(
            P(None, "wide"),
            P("wide"),
            P("wide", "seq"),
            P("wide", None, "seq"),
            P("seq", "wide"),
            P(),
            P(),
            P(None, ("seq", "wide"), None, None),
            P(None, ("seq", "wide"), None, None),
            P(),
        ),
        out_specs=P(None, "wide"),
        check_vma=False,
    )
```

```python
import math

import jax
import jax.numpy as jnp
import numpy as np
from jax import lax
from jax.experimental import pallas as pl
from jax.experimental.pallas import tpu as pltpu
from jax.sharding import PartitionSpec as P

rope_base = 1000000.0
eps_norm = 1e-06
neg_large = -1e30
MESH = pl.DeviceIdType.MESH
f32 = jnp.float32
bf16 = jnp.bfloat16

ROWS, KVH, GROUP, HD = 8, 8, 8, 128
HEADS = KVH * GROUP
BLOCK = 512
FLAT = BLOCK * KVH
NSEQ, NWIDE = 8, 16
WIDTH = 320
D = 5120


def lane_iota(shape):
    return lax.broadcasted_iota(jnp.int32, shape, len(shape) - 1)


def kernel(
    x_hbm, gain_hbm, wq_hbm, wkv_hbm, wo_hbm, qg_hbm, kg_hbm, k_hbm, v_hbm, freq_hbm, len_ref,
    out_ref,
    x_v, gain_v, wq_v, wkv_v, wo_v, qg_v, kg_v, k_v, v_v, freq_v,
    k_t, v_r, s1, r1, skv, rkv, sq, qall, qf, qt, knew, vnew, scr, pb,
    s3, r3, s4, r4, of, s5, r5,
    in_sem, k_sem, v_sem, ssem, rsem,
):
    s = lax.axis_index("seq")
    w = lax.axis_index("wide")
    x = w // 4
    yh = (w // 2) % 2
    core = w % 2
    yl = s // 4
    z = s % 4

    small = [
        pltpu.make_async_copy(a, b, in_sem.at[i])
        for i, (a, b) in enumerate(
            [
                (x_hbm, x_v),
                (gain_hbm, gain_v),
                (wq_hbm, wq_v),
                (qg_hbm, qg_v),
                (kg_hbm, kg_v),
                (freq_hbm, freq_v),
                (wkv_hbm, wkv_v),
                (wo_hbm, wo_v),
            ]
        )
    ]
    for c in small[:6]:
        c.start()

    def ring(k):
        return min(k, 4 - k)

    def y_hops(hi, lo):
        return 1 if lo else 2 * hi

    steps = [(kx, hi, kc) for kx in range(4) for hi in range(2) for kc in range(2)]
    steps.sort(key=lambda k: (-ring(k[0]) - y_hops(k[1], 0), -k[2]))
    wide_to = [
        ((x + kx) % 4) * 4 + ((yh + hi) % 2) * 2 + (core + kc) % 2
        for kx, hi, kc in steps
        if kx or hi or kc
    ]
    steps = [
        (kz, hi, lo, kc)
        for kz in range(4)
        for hi in range(2)
        for lo in range(2)
        for kc in range(2)
    ]
    steps.sort(key=lambda k: (-ring(k[0]) - y_hops(k[1], k[2]), -k[3]))
    plane_to = [
        (
            ((yl + lo) % 2) * 4 + (z + kz) % 4,
            x * 4 + ((yh + hi) % 2) * 2 + (core + kc) % 2,
            bool(kz or lo),
        )
        for kz, hi, lo, kc in steps
        if kz or hi or lo or kc
    ]
    steps = [(kz, lo) for kz in range(4) for lo in range(2)]
    steps.sort(key=lambda k: -ring(k[0]) - k[1])
    seq_to = [((yl + lo) % 2) * 4 + (z + kz) % 4 for kz, lo in steps if kz or lo]

    bar = pltpu.get_barrier_semaphore()
    n_bar = 0
    for tw in wide_to:
        pl.semaphore_signal(bar, inc=1, device_id=(s, tw), device_id_type=MESH)
        n_bar += 1
    for ts, tw, far in plane_to:
        if far:
            pl.semaphore_signal(bar, inc=1, device_id=(ts, tw), device_id_type=MESH)
            n_bar += 1

    def remote(src, dst, i, to):
        return pltpu.make_async_remote_copy(
            src_ref=src, dst_ref=dst, send_sem=ssem.at[i], recv_sem=rsem.at[i],
            device_id=to, device_id_type=MESH,
        )

    for c in small[6:]:
        c.start()
    k_cp = [pltpu.make_async_copy(k_hbm.at[b], k_v.at[b], k_sem.at[b]) for b in range(ROWS)]
    v_cp = [pltpu.make_async_copy(v_hbm.at[b], v_v.at[b], v_sem.at[b]) for b in range(ROWS)]
    for c in k_cp + v_cp:
        c.start()

    for c in small[:6]:
        c.wait()
    xf = x_v[...].astype(f32)
    ss = jnp.sum(xf * xf, axis=-1, keepdims=True)
    normed = (xf * gain_v[...][None, :]).astype(bf16)
    row = lax.broadcasted_iota(jnp.int32, (ROWS, HD), 0)
    lane = lane_iota((ROWS, HD))
    ss_row = jnp.sum(jnp.where(lane == row, ss, 0.0), axis=0, keepdims=True)
    for p in range(4):
        part = jnp.dot(normed, wq_v[:, p * 256 : (p + 1) * 256], preferred_element_type=f32)
        s1[p, 0:ROWS] = part[:, :HD]
        s1[p, ROWS : 2 * ROWS] = part[:, HD:]
        s1[p, 2 * ROWS : 2 * ROWS + 1] = ss_row
    r1[w] = s1[w % 4]

    def turn_k(b, carry):
        pltpu.make_async_copy(k_hbm.at[b], k_v.at[b], k_sem.at[b]).wait()
        for ch in range(2):
            part = k_v[b, pl.ds(ch * 2048, 2048), :].reshape(256, KVH, HD).reshape(256, KVH * HD)
            k_t[b, :, ch * 256 : (ch + 1) * 256] = part.T
        return carry

    def turn_v(b, carry):
        pltpu.make_async_copy(v_hbm.at[b], v_v.at[b], v_sem.at[b]).wait()
        for ch in range(2):
            part = v_v[b, pl.ds(ch * 2048, 2048), :].reshape(256, KVH, HD)
            v_r[b, pl.ds(ch * 256, 256), :] = part.reshape(256, KVH * HD)
        return carry

    pl.semaphore_wait(bar, n_bar)
    for tw in wide_to:
        remote(s1.at[tw % 4], r1.at[w], 0, (s, tw)).start()

    small[6].wait()
    row_i = lax.broadcasted_iota(jnp.int32, (WIDTH, 2 * WIDTH), 0)
    col_i = lax.broadcasted_iota(jnp.int32, (WIDTH, 2 * WIDTH), 1)
    spread = jnp.where(col_i // 2 == row_i, 1.0, 0.0).astype(bf16)
    twice = jnp.dot(normed, spread, preferred_element_type=f32)
    odd = lane_iota((ROWS, 2 * WIDTH)) % 2
    both = jnp.concatenate(
        [jnp.where(odd == 0, twice, 0.0), jnp.where(odd == 1, twice, 0.0)], axis=0
    ).astype(bf16)
    kv_part = jnp.dot(both, wkv_v[...], preferred_element_type=f32)
    skv[0] = kv_part[:ROWS]
    skv[1] = kv_part[ROWS:]

    lens = jnp.zeros((ROWS, HD), jnp.int32)
    for b in range(ROWS):
        lens = jnp.where(row == b, len_ref[b], lens)
    angle = lens.astype(f32) * freq_v[...]
    cosine = jnp.cos(angle)
    sine = jnp.where(lane < HD // 2, -jnp.sin(angle), jnp.sin(angle))

    def head(u, inv_rms, gain):
        mean = jnp.mean(u * u, axis=-1, keepdims=True) * (inv_rms * inv_rms)
        u = u * gain * (inv_rms * lax.rsqrt(mean + eps_norm))
        return u * cosine + pltpu.roll(u, HD // 2, 1) * sine

    for t in range(2):

        @pl.when(w != t)
        def _():
            remote(skv, rkv.at[w], 1, (s, t)).start()

        @pl.when(w == t)
        def _():
            rkv[w] = skv[...]

    lax.fori_loop(0, 4, turn_k, 0)

    remote(r1.at[pl.ds(0, NWIDE - 1)], r1.at[pl.ds(0, NWIDE - 1)], 0, (s, w)).wait_recv()
    tot = r1[0]
    for i in range(1, NWIDE):
        tot = tot + r1[i]
    ss = jnp.sum(
        jnp.where(lane == row, tot[2 * ROWS : 2 * ROWS + 1], 0.0), axis=-1, keepdims=True
    )
    inv_rms = lax.rsqrt(ss / D + eps_norm)
    sq[...] = jnp.concatenate(
        [head(tot[:ROWS], inv_rms, qg_v[...]), head(tot[ROWS : 2 * ROWS], inv_rms, qg_v[...])],
        axis=0,
    ).astype(bf16)

    p_own = w % 4
    for ts, tw, _far in plane_to:
        remote(sq, qall.at[s * 4 + p_own], 2, (ts, tw)).start()
    qall[s * 4 + p_own] = sq[...]

    lax.fori_loop(4, ROWS, turn_k, 0)
    lax.fori_loop(0, ROWS, turn_v, 0)

    remote(qall.at[pl.ds(0, 31)], qall.at[pl.ds(0, 31)], 2, (s, w)).wait_recv()
    qf[...] = qall[...].reshape(HEADS * ROWS, HD).astype(f32)
    for b in range(ROWS):
        qt[b] = qf[pl.ds(b, HEADS, stride=ROWS), :]

    scale = HD ** (-0.5)
    start = (s * NWIDE + w) * BLOCK
    plane = lane_iota((HEADS, BLOCK))
    none = jnp.zeros((GROUP, HD), f32)
    block32 = lane_iota((HEADS, HD)) // 32
    low = lane_iota((HEADS, HD)) % 32 < 16
    low16 = lane % 32 < 16

    def by_block(parts):
        n = parts[0].shape[0]
        out = parts[0]
        for i in range(1, 4):
            out = jnp.where(block32[:n] == i, parts[i], out)
        return out

    def pack(peak, total):
        high = total.astype(bf16).astype(f32)
        n = low[: peak.shape[0]]
        return jnp.where(n, peak, high), jnp.where(n, 0.0, total - high)

    slot3 = s * 2 + core
    for c in range(2):
        rows = range(c * 4, c * 4 + 4)
        scores, peaks, totals, weights, numers = {}, {}, {}, {}, {}
        for b in rows:
            parts = []
            for pr in range(4):
                one = qt[b, 16 * pr : 16 * pr + 8, :]
                two = qt[b, 16 * pr + 8 : 16 * pr + 16, :]
                lhs = jnp.concatenate(
                    [jnp.concatenate([one, none], axis=1), jnp.concatenate([none, two], axis=1)],
                    axis=0,
                ).astype(bf16)
                keys = k_t[b, pr * 256 : (pr + 1) * 256, :]
                parts.append(jnp.dot(lhs, keys, preferred_element_type=f32))
            scr[b % 4] = jnp.concatenate(parts, axis=0)
        for b in rows:
            valid = plane < len_ref[b] - start
            t = jnp.where(valid, scr[b % 4] * scale, neg_large)
            m = jnp.max(t, axis=-1, keepdims=True).astype(bf16).astype(f32)
            e = jnp.where(valid, jnp.exp(t - m), 0.0)
            peaks[b] = jnp.broadcast_to(m, (HEADS, HD))
            totals[b] = jnp.broadcast_to(jnp.sum(e, axis=-1, keepdims=True), (HEADS, HD))
            pb[b % 4] = e.astype(bf16)
        for b in rows:
            for pr in range(4):
                n = jnp.dot(
                    pb[b % 4, 16 * pr : 16 * pr + 16, :],
                    v_r[b, :, pr * 256 : (pr + 1) * 256],
                    preferred_element_type=f32,
                )
                numers[b, 2 * pr] = n[:GROUP, :HD]
                numers[b, 2 * pr + 1] = n[GROUP:, HD:]
        stats = pack(by_block([peaks[b] for b in rows]), by_block([totals[b] for b in rows]))
        for g in range(KVH):
            own = slice(g * GROUP, (g + 1) * GROUP)
            s3[c, g] = jnp.concatenate(
                [numers[b, g] for b in rows] + [part[own] for part in stats], axis=0
            ).astype(bf16)
        tw = w - core + c
        for ts in seq_to:
            remote(s3.at[c, ts], r3.at[slot3], 3, (ts, tw)).start()

        @pl.when(core != c)
        def _():
            remote(s3.at[c, s], r3.at[slot3], 3, (s, tw)).start()

        @pl.when(core == c)
        def _():
            r3[slot3] = s3[c, s]

    @pl.when(w < 2)
    def _():
        remote(rkv.at[pl.ds(0, NWIDE - 1)], rkv.at[pl.ds(0, NWIDE - 1)], 1, (s, w)).wait_recv()
        kv = rkv[0]
        for i in range(1, NWIDE):
            kv = kv + rkv[i]
        knew[...] = head(kv[0], inv_rms, kg_v[...]).astype(bf16).astype(f32)
        vnew[...] = (kv[1] * inv_rms).astype(bf16).astype(f32)

    @pl.when(w < 2)
    def _():
        peaks, totals, numers = [], [], []
        for i in range(4):
            b = core * 4 + i
            qrow = qt[b, pl.ds(s * GROUP, GROUP), :]
            sn = jnp.sum(qrow * knew[pl.ds(b, 1), :], axis=-1, keepdims=True) * scale
            sn = jnp.broadcast_to(sn, (GROUP, HD))
            mn = sn.astype(bf16).astype(f32)
            pn = jnp.exp(sn - mn)
            peaks.append(mn)
            totals.append(pn)
            numers.append(pn.astype(bf16).astype(f32) * vnew[pl.ds(b, 1), :])
        r3[16] = jnp.concatenate(
            numers + list(pack(by_block(peaks), by_block(totals))), axis=0
        ).astype(bf16)

    @pl.when(w >= 2)
    def _():
        r3[16] = jnp.concatenate(
            [jnp.zeros((32, HD), f32)]
            + list(pack(jnp.full((GROUP, HD), neg_large, f32), jnp.zeros((GROUP, HD), f32))),
            axis=0,
        ).astype(bf16)

    remote(r3.at[pl.ds(0, 15)], r3.at[pl.ds(0, 15)], 3, (s, w)).wait_recv()

    def merge(messages):
        messages = [msg.astype(f32) for msg in messages]
        high = [msg[32:40] for msg in messages]
        peak = high[0]
        for t in high[1:]:
            peak = jnp.maximum(peak, t)
        total = jnp.zeros((GROUP, HD), f32)
        acc = [jnp.zeros((GROUP, HD), f32) for _ in range(4)]
        for t, msg in zip(high, messages):
            f = jnp.exp(t - peak)
            total = total + f * pltpu.roll(t + msg[40:48], HD - 16, 1)
            for i in range(4):
                acc[i] = acc[i] + jnp.broadcast_to(f[:, 32 * i : 32 * i + 1], (GROUP, HD)) * msg[
                    i * GROUP : (i + 1) * GROUP
                ]
        return peak, total, acc

    peak, total, acc = merge([r3[i] for i in range(17)])
    s4[...] = jnp.concatenate(acc + list(pack(peak, pltpu.roll(total, 16, 1))), axis=0).astype(bf16)
    for tw in wide_to:
        remote(s4, r4.at[w], 5, (s, tw)).start()
    r4[w] = s4[...]
    small[7].wait()
    remote(r4.at[pl.ds(0, 15)], r4.at[pl.ds(0, 15)], 5, (s, w)).wait_recv()
    for c in range(2):
        peak, total, acc = merge([r4[2 * i + c] for i in range(8)])
        for i in range(4):
            den = jnp.broadcast_to(total[:, 32 * i : 32 * i + 1], (GROUP, HD))
            of[pl.ds((c * 4 + i) * GROUP, GROUP), :] = acc[i] / den

    o = jnp.concatenate(
        [of[pl.ds(j, ROWS, stride=GROUP), :].astype(bf16) for j in range(GROUP)], axis=1
    )
    s5[...] = lax.dot_general(o, wo_v[...], (((1,), (1,)), ((), ())), preferred_element_type=f32)
    for ts in seq_to:
        remote(s5, r5.at[s], 7, (ts, w)).start()
    r5[s] = s5[...]
    remote(r5.at[pl.ds(0, 7)], r5.at[pl.ds(0, 7)], 7, (s, w)).wait_recv()
    out = r5[0]
    for i in range(1, NSEQ):
        out = out + r5[i]
    out_ref[...] = out

    remote(r1.at[pl.ds(0, 15)], r1.at[pl.ds(0, 15)], 0, (s, w)).wait_send()
    for t in range(2):

        @pl.when(w != t)
        def _():
            remote(skv, rkv.at[w], 1, (s, t)).wait_send()

    remote(qall.at[pl.ds(0, 31)], qall.at[pl.ds(0, 31)], 2, (s, w)).wait_send()
    remote(r3.at[pl.ds(0, 15)], r3.at[pl.ds(0, 15)], 3, (s, w)).wait_send()
    remote(r4.at[pl.ds(0, 15)], r4.at[pl.ds(0, 15)], 5, (s, w)).wait_send()
    remote(r5.at[pl.ds(0, 7)], r5.at[pl.ds(0, 7)], 7, (s, w)).wait_send()


def body(
    activations, attn_gain, w_query, w_keyval, w_output, query_gain, key_gain, key_cache, value_cache, lengths
):
    half = HD // 2
    freq = np.exp(-(2.0 * np.arange(half) / HD) * math.log(rope_base)).astype(np.float32)
    freq = jnp.asarray(np.concatenate([freq, freq])[None, :])
    any_spec = pl.BlockSpec(memory_space=pl.ANY)
    vm = pltpu.VMEM
    return pl.pallas_call(
        kernel,
        out_shape=pltpu.VMEM((ROWS, WIDTH), f32),
        in_specs=[any_spec] * 10 + [pl.BlockSpec(memory_space=pltpu.SMEM)],
        out_specs=pl.BlockSpec(memory_space=pltpu.VMEM),
        scratch_shapes=[
            vm((ROWS, WIDTH), bf16),
            vm((WIDTH,), f32),
            vm((WIDTH, 1024), bf16),
            vm((2 * WIDTH, HD), bf16),
            vm((WIDTH, 1024), bf16),
            vm((1, HD), f32),
            vm((1, HD), f32),
            vm((ROWS, FLAT, HD), bf16),
            vm((ROWS, FLAT, HD), bf16),
            vm((1, HD), f32),
            vm((ROWS, KVH * HD, BLOCK), bf16),
            vm((ROWS, BLOCK, KVH * HD), bf16),
            vm((4, 17, HD), f32),
            vm((NWIDE, 17, HD), f32),
            vm((2, ROWS, HD), f32),
            vm((NWIDE, 2, ROWS, HD), f32),
            vm((16, HD), bf16),
            vm((32, 16, HD), bf16),
            vm((HEADS * ROWS, HD), f32),
            vm((ROWS, HEADS, HD), f32),
            vm((ROWS, HD), f32),
            vm((ROWS, HD), f32),
            vm((4, HEADS, BLOCK), f32),
            vm((4, HEADS, BLOCK), bf16),
            vm((2, KVH, 48, HD), bf16),
            vm((17, 48, HD), bf16),
            vm((48, HD), bf16),
            vm((NWIDE, 48, HD), bf16),
            vm((HEADS, HD), f32),
            vm((ROWS, WIDTH), f32),
            vm((NSEQ, ROWS, WIDTH), f32),
            pltpu.SemaphoreType.DMA((8,)),
            pltpu.SemaphoreType.DMA((ROWS,)),
            pltpu.SemaphoreType.DMA((ROWS,)),
            pltpu.SemaphoreType.DMA((8,)),
            pltpu.SemaphoreType.DMA((8,)),
        ],
        compiler_params=pltpu.CompilerParams(
            collective_id=0, has_side_effects=True, vmem_limit_bytes=60 * 1024 * 1024
        ),
    )(
        activations,
        attn_gain,
        w_query,
        w_keyval.reshape(2 * WIDTH, HD),
        w_output.T,
        query_gain.reshape(1, HD),
        key_gain.reshape(1, HD),
        key_cache.reshape(ROWS, FLAT, HD),
        value_cache.reshape(ROWS, FLAT, HD),
        freq,
        lengths,
    )


def solution(mesh):
    return jax.shard_map(
        body,
        mesh=mesh,
        in_specs=(
            P(None, "wide"),
            P("wide"),
            P("wide", "seq"),
            P("wide", None, "seq"),
            P("seq", "wide"),
            P(),
            P(),
            P(None, ("seq", "wide"), None, None),
            P(None, ("seq", "wide"), None, None),
            P(),
        ),
        out_specs=P(None, "wide"),
        check_vma=False,
    )
```

```python
import math

import jax
import jax.numpy as jnp
import numpy as np
from jax import lax
from jax.experimental import pallas as pl
from jax.experimental.pallas import tpu as pltpu
from jax.sharding import PartitionSpec as P

rope_base = 1000000.0
eps_norm = 1e-06
neg_large = -1e30
MESH = pl.DeviceIdType.MESH
f32 = jnp.float32
bf16 = jnp.bfloat16

ROWS, KVH, GROUP, HD = 8, 8, 8, 128
HEADS = KVH * GROUP
BLOCK = 512
FLAT = BLOCK * KVH
NSEQ, NWIDE = 8, 16
WIDTH = 320
D = 5120


def lane_iota(shape):
    return lax.broadcasted_iota(jnp.int32, shape, len(shape) - 1)


def kernel(
    x_hbm, gain_hbm, wq_hbm, wkv_hbm, wo_hbm, qg_hbm, kg_hbm, k_hbm, v_hbm, freq_hbm, len_hbm,
    out_ref,
    x_v, gain_v, wq_v, wkv_v, wo_v, qg_v, kg_v, k_v, v_v, freq_v,
    len_ref, k_t, v_r, s1, r1, skv, rkv, sq, qall, qf, qt, knew, vnew, scr, pb,
    s3, r3, s4, r4, of, s5, r5,
    in_sem, k_sem, v_sem, ssem, rsem,
):
    s = lax.axis_index("seq")
    w = lax.axis_index("wide")
    x = w // 4
    yh = (w // 2) % 2
    core = w % 2
    yl = s // 4
    z = s % 4

    small = [
        pltpu.make_async_copy(a, b, in_sem.at[i])
        for i, (a, b) in enumerate(
            [
                (x_hbm, x_v),
                (gain_hbm, gain_v),
                (wq_hbm, wq_v),
                (qg_hbm, qg_v),
                (kg_hbm, kg_v),
                (freq_hbm, freq_v),
                (wkv_hbm, wkv_v),
                (wo_hbm, wo_v),
                (len_hbm, len_ref),
            ]
        )
    ]

    def ring(k):
        return min(k, 4 - k)

    def y_hops(hi, lo):
        return 1 if lo else 2 * hi

    steps = [(kx, hi, kc) for kx in range(4) for hi in range(2) for kc in range(2)]
    steps.sort(key=lambda k: (-ring(k[0]) - y_hops(k[1], 0), -k[2]))
    wide_to = [
        ((x + kx) % 4) * 4 + ((yh + hi) % 2) * 2 + (core + kc) % 2
        for kx, hi, kc in steps
        if kx or hi or kc
    ]
    steps = [
        (kz, hi, lo, kc)
        for kz in range(4)
        for hi in range(2)
        for lo in range(2)
        for kc in range(2)
    ]
    steps.sort(key=lambda k: (-ring(k[0]) - y_hops(k[1], k[2]), -k[3]))
    plane_to = [
        (
            ((yl + lo) % 2) * 4 + (z + kz) % 4,
            x * 4 + ((yh + hi) % 2) * 2 + (core + kc) % 2,
            bool(kz or lo),
        )
        for kz, hi, lo, kc in steps
        if kz or hi or lo or kc
    ]
    steps = [(kz, lo) for kz in range(4) for lo in range(2)]
    steps.sort(key=lambda k: -ring(k[0]) - k[1])
    seq_to = [((yl + lo) % 2) * 4 + (z + kz) % 4 for kz, lo in steps if kz or lo]

    for c in small[:3]:
        c.start()
    bar = pltpu.get_barrier_semaphore()
    n_bar = 0
    for tw in wide_to:
        pl.semaphore_signal(bar, inc=1, device_id=(s, tw), device_id_type=MESH)
        n_bar += 1
    for ts, tw, far in plane_to:
        if far:
            pl.semaphore_signal(bar, inc=1, device_id=(ts, tw), device_id_type=MESH)
            n_bar += 1

    def remote(src, dst, i, to):
        return pltpu.make_async_remote_copy(
            src_ref=src, dst_ref=dst, send_sem=ssem.at[i], recv_sem=rsem.at[i],
            device_id=to, device_id_type=MESH,
        )

    for c in small[3:]:
        c.start()
    k_cp = [pltpu.make_async_copy(k_hbm.at[b], k_v.at[b], k_sem.at[b]) for b in range(ROWS)]
    v_cp = [pltpu.make_async_copy(v_hbm.at[b], v_v.at[b], v_sem.at[b]) for b in range(ROWS)]
    for c in k_cp + v_cp:
        c.start()

    for c in small[:3]:
        c.wait()
    xf = x_v[...].astype(f32)
    ss = jnp.sum(xf * xf, axis=-1, keepdims=True)
    normed = (xf * gain_v[...][None, :]).astype(bf16)
    row = lax.broadcasted_iota(jnp.int32, (ROWS, HD), 0)
    lane = lane_iota((ROWS, HD))
    ss_row = jnp.sum(jnp.where(lane == row, ss, 0.0), axis=0, keepdims=True)
    for p in range(4):
        part = jnp.dot(normed, wq_v[:, p * 256 : (p + 1) * 256], preferred_element_type=f32)
        s1[p, 0:ROWS] = part[:, :HD]
        s1[p, ROWS : 2 * ROWS] = part[:, HD:]
        s1[p, 2 * ROWS : 2 * ROWS + 1] = ss_row
    r1[w] = s1[w % 4]

    def turn_k(b, carry):
        pltpu.make_async_copy(k_hbm.at[b], k_v.at[b], k_sem.at[b]).wait()
        for ch in range(2):
            part = k_v[b, pl.ds(ch * 2048, 2048), :].reshape(256, KVH, HD).reshape(256, KVH * HD)
            k_t[b, :, ch * 256 : (ch + 1) * 256] = part.T
        return carry

    def turn_v(b, carry):
        pltpu.make_async_copy(v_hbm.at[b], v_v.at[b], v_sem.at[b]).wait()
        for ch in range(2):
            part = v_v[b, pl.ds(ch * 2048, 2048), :].reshape(256, KVH, HD)
            v_r[b, pl.ds(ch * 256, 256), :] = part.reshape(256, KVH * HD)
        return carry

    pl.semaphore_wait(bar, n_bar)
    for tw in wide_to:
        remote(s1.at[tw % 4], r1.at[w], 0, (s, tw)).start()

    for c in small[3:7]:
        c.wait()
    row_i = lax.broadcasted_iota(jnp.int32, (WIDTH, 2 * WIDTH), 0)
    col_i = lax.broadcasted_iota(jnp.int32, (WIDTH, 2 * WIDTH), 1)
    spread = jnp.where(col_i // 2 == row_i, 1.0, 0.0).astype(bf16)
    twice = jnp.dot(normed, spread, preferred_element_type=f32)
    odd = lane_iota((ROWS, 2 * WIDTH)) % 2
    both = jnp.concatenate(
        [jnp.where(odd == 0, twice, 0.0), jnp.where(odd == 1, twice, 0.0)], axis=0
    ).astype(bf16)
    kv_part = jnp.dot(both, wkv_v[...], preferred_element_type=f32)
    skv[0] = kv_part[:ROWS]
    skv[1] = kv_part[ROWS:]

    small[8].wait()
    lens = jnp.zeros((ROWS, HD), jnp.int32)
    for b in range(ROWS):
        lens = jnp.where(row == b, len_ref[b], lens)
    angle = lens.astype(f32) * freq_v[...]
    cosine = jnp.cos(angle)
    sine = jnp.where(lane < HD // 2, -jnp.sin(angle), jnp.sin(angle))

    def head(u, inv_rms, gain):
        mean = jnp.mean(u * u, axis=-1, keepdims=True) * (inv_rms * inv_rms)
        u = u * gain * (inv_rms * lax.rsqrt(mean + eps_norm))
        return u * cosine + pltpu.roll(u, HD // 2, 1) * sine

    for t in range(2):

        @pl.when(w != t)
        def _():
            remote(skv, rkv.at[w], 1, (s, t)).start()

        @pl.when(w == t)
        def _():
            rkv[w] = skv[...]

    lax.fori_loop(0, 4, turn_k, 0)

    remote(r1.at[pl.ds(0, NWIDE - 1)], r1.at[pl.ds(0, NWIDE - 1)], 0, (s, w)).wait_recv()
    tot = r1[0]
    for i in range(1, NWIDE):
        tot = tot + r1[i]
    ss = jnp.sum(
        jnp.where(lane == row, tot[2 * ROWS : 2 * ROWS + 1], 0.0), axis=-1, keepdims=True
    )
    inv_rms = lax.rsqrt(ss / D + eps_norm)
    sq[...] = jnp.concatenate(
        [head(tot[:ROWS], inv_rms, qg_v[...]), head(tot[ROWS : 2 * ROWS], inv_rms, qg_v[...])],
        axis=0,
    ).astype(bf16)

    p_own = w % 4
    for ts, tw, _far in plane_to:
        remote(sq, qall.at[s * 4 + p_own], 2, (ts, tw)).start()
    qall[s * 4 + p_own] = sq[...]

    lax.fori_loop(4, ROWS, turn_k, 0)
    lax.fori_loop(0, ROWS, turn_v, 0)

    remote(qall.at[pl.ds(0, 31)], qall.at[pl.ds(0, 31)], 2, (s, w)).wait_recv()
    qf[...] = qall[...].reshape(HEADS * ROWS, HD).astype(f32)
    for b in range(ROWS):
        qt[b] = qf[pl.ds(b, HEADS, stride=ROWS), :]

    scale = HD ** (-0.5)
    start = (s * NWIDE + w) * BLOCK
    plane = lane_iota((HEADS, BLOCK))
    none = jnp.zeros((GROUP, HD), f32)
    block32 = lane_iota((HEADS, HD)) // 32
    low = lane_iota((HEADS, HD)) % 32 < 16
    low16 = lane % 32 < 16

    def by_block(parts):
        n = parts[0].shape[0]
        out = parts[0]
        for i in range(1, 4):
            out = jnp.where(block32[:n] == i, parts[i], out)
        return out

    def pack(peak, total):
        high = total.astype(bf16).astype(f32)
        n = low[: peak.shape[0]]
        return jnp.where(n, peak, high), jnp.where(n, 0.0, total - high)

    slot3 = s * 2 + core
    for c in range(2):
        rows = range(c * 4, c * 4 + 4)
        scores, peaks, totals, weights, numers = {}, {}, {}, {}, {}
        for b in rows:
            parts = []
            for pr in range(4):
                one = qt[b, 16 * pr : 16 * pr + 8, :]
                two = qt[b, 16 * pr + 8 : 16 * pr + 16, :]
                lhs = jnp.concatenate(
                    [jnp.concatenate([one, none], axis=1), jnp.concatenate([none, two], axis=1)],
                    axis=0,
                ).astype(bf16)
                keys = k_t[b, pr * 256 : (pr + 1) * 256, :]
                parts.append(jnp.dot(lhs, keys, preferred_element_type=f32))
            scr[b % 4] = jnp.concatenate(parts, axis=0)
        for b in rows:
            valid = plane < len_ref[b] - start
            t = jnp.where(valid, scr[b % 4] * scale, neg_large)
            m = jnp.max(t, axis=-1, keepdims=True).astype(bf16).astype(f32)
            e = jnp.where(valid, jnp.exp(t - m), 0.0)
            peaks[b] = jnp.broadcast_to(m, (HEADS, HD))
            totals[b] = jnp.broadcast_to(jnp.sum(e, axis=-1, keepdims=True), (HEADS, HD))
            pb[b % 4] = e.astype(bf16)
        for b in rows:
            for pr in range(4):
                n = jnp.dot(
                    pb[b % 4, 16 * pr : 16 * pr + 16, :],
                    v_r[b, :, pr * 256 : (pr + 1) * 256],
                    preferred_element_type=f32,
                )
                numers[b, 2 * pr] = n[:GROUP, :HD]
                numers[b, 2 * pr + 1] = n[GROUP:, HD:]
        stats = pack(by_block([peaks[b] for b in rows]), by_block([totals[b] for b in rows]))
        for g in range(KVH):
            own = slice(g * GROUP, (g + 1) * GROUP)
            s3[c, g] = jnp.concatenate(
                [numers[b, g] for b in rows] + [part[own] for part in stats], axis=0
            ).astype(bf16)
        tw = w - core + c
        for ts in seq_to:
            remote(s3.at[c, ts], r3.at[slot3], 3, (ts, tw)).start()

        @pl.when(core != c)
        def _():
            remote(s3.at[c, s], r3.at[slot3], 3, (s, tw)).start()

        @pl.when(core == c)
        def _():
            r3[slot3] = s3[c, s]

    @pl.when(w < 2)
    def _():
        remote(rkv.at[pl.ds(0, NWIDE - 1)], rkv.at[pl.ds(0, NWIDE - 1)], 1, (s, w)).wait_recv()
        kv = rkv[0]
        for i in range(1, NWIDE):
            kv = kv + rkv[i]
        knew[...] = head(kv[0], inv_rms, kg_v[...]).astype(bf16).astype(f32)
        vnew[...] = (kv[1] * inv_rms).astype(bf16).astype(f32)

    @pl.when(w < 2)
    def _():
        peaks, totals, numers = [], [], []
        for i in range(4):
            b = core * 4 + i
            qrow = qt[b, pl.ds(s * GROUP, GROUP), :]
            sn = jnp.sum(qrow * knew[pl.ds(b, 1), :], axis=-1, keepdims=True) * scale
            sn = jnp.broadcast_to(sn, (GROUP, HD))
            mn = sn.astype(bf16).astype(f32)
            pn = jnp.exp(sn - mn)
            peaks.append(mn)
            totals.append(pn)
            numers.append(pn.astype(bf16).astype(f32) * vnew[pl.ds(b, 1), :])
        r3[16] = jnp.concatenate(
            numers + list(pack(by_block(peaks), by_block(totals))), axis=0
        ).astype(bf16)

    @pl.when(w >= 2)
    def _():
        r3[16] = jnp.concatenate(
            [jnp.zeros((32, HD), f32)]
            + list(pack(jnp.full((GROUP, HD), neg_large, f32), jnp.zeros((GROUP, HD), f32))),
            axis=0,
        ).astype(bf16)

    remote(r3.at[pl.ds(0, 15)], r3.at[pl.ds(0, 15)], 3, (s, w)).wait_recv()

    def merge(messages):
        messages = [msg.astype(f32) for msg in messages]
        high = [msg[32:40] for msg in messages]
        peak = high[0]
        for t in high[1:]:
            peak = jnp.maximum(peak, t)
        total = jnp.zeros((GROUP, HD), f32)
        acc = [jnp.zeros((GROUP, HD), f32) for _ in range(4)]
        for t, msg in zip(high, messages):
            f = jnp.exp(t - peak)
            total = total + f * pltpu.roll(t + msg[40:48], HD - 16, 1)
            for i in range(4):
                acc[i] = acc[i] + jnp.broadcast_to(f[:, 32 * i : 32 * i + 1], (GROUP, HD)) * msg[
                    i * GROUP : (i + 1) * GROUP
                ]
        return peak, total, acc

    peak, total, acc = merge([r3[i] for i in range(17)])
    s4[...] = jnp.concatenate(acc + list(pack(peak, pltpu.roll(total, 16, 1))), axis=0).astype(bf16)
    for tw in wide_to:
        remote(s4, r4.at[w], 5, (s, tw)).start()
    r4[w] = s4[...]
    small[7].wait()
    remote(r4.at[pl.ds(0, 15)], r4.at[pl.ds(0, 15)], 5, (s, w)).wait_recv()
    for c in range(2):
        peak, total, acc = merge([r4[2 * i + c] for i in range(8)])
        for i in range(4):
            den = jnp.broadcast_to(total[:, 32 * i : 32 * i + 1], (GROUP, HD))
            of[pl.ds((c * 4 + i) * GROUP, GROUP), :] = acc[i] / den

    o = jnp.concatenate(
        [of[pl.ds(j, ROWS, stride=GROUP), :].astype(bf16) for j in range(GROUP)], axis=1
    )
    s5[...] = lax.dot_general(o, wo_v[...], (((1,), (1,)), ((), ())), preferred_element_type=f32)
    for ts in seq_to:
        remote(s5, r5.at[s], 7, (ts, w)).start()
    r5[s] = s5[...]
    remote(r5.at[pl.ds(0, 7)], r5.at[pl.ds(0, 7)], 7, (s, w)).wait_recv()
    out = r5[0]
    for i in range(1, NSEQ):
        out = out + r5[i]
    out_ref[...] = out

    remote(r1.at[pl.ds(0, 15)], r1.at[pl.ds(0, 15)], 0, (s, w)).wait_send()
    for t in range(2):

        @pl.when(w != t)
        def _():
            remote(skv, rkv.at[w], 1, (s, t)).wait_send()

    remote(qall.at[pl.ds(0, 31)], qall.at[pl.ds(0, 31)], 2, (s, w)).wait_send()
    remote(r3.at[pl.ds(0, 15)], r3.at[pl.ds(0, 15)], 3, (s, w)).wait_send()
    remote(r4.at[pl.ds(0, 15)], r4.at[pl.ds(0, 15)], 5, (s, w)).wait_send()
    remote(r5.at[pl.ds(0, 7)], r5.at[pl.ds(0, 7)], 7, (s, w)).wait_send()


def body(
    activations, attn_gain, w_query, w_keyval, w_output, query_gain, key_gain, key_cache, value_cache, lengths
):
    half = HD // 2
    freq = np.exp(-(2.0 * np.arange(half) / HD) * math.log(rope_base)).astype(np.float32)
    freq = jnp.asarray(np.concatenate([freq, freq])[None, :])
    any_spec = pl.BlockSpec(memory_space=pl.ANY)
    vm = pltpu.VMEM
    return pl.pallas_call(
        kernel,
        out_shape=pltpu.VMEM((ROWS, WIDTH), f32),
        in_specs=[any_spec] * 11,
        out_specs=pl.BlockSpec(memory_space=pltpu.VMEM),
        scratch_shapes=[
            vm((ROWS, WIDTH), bf16),
            vm((WIDTH,), f32),
            vm((WIDTH, 1024), bf16),
            vm((2 * WIDTH, HD), bf16),
            vm((WIDTH, 1024), bf16),
            vm((1, HD), f32),
            vm((1, HD), f32),
            vm((ROWS, FLAT, HD), bf16),
            vm((ROWS, FLAT, HD), bf16),
            vm((1, HD), f32),
            pltpu.SMEM((ROWS,), jnp.int32),
            vm((ROWS, KVH * HD, BLOCK), bf16),
            vm((ROWS, BLOCK, KVH * HD), bf16),
            vm((4, 17, HD), f32),
            vm((NWIDE, 17, HD), f32),
            vm((2, ROWS, HD), f32),
            vm((NWIDE, 2, ROWS, HD), f32),
            vm((16, HD), bf16),
            vm((32, 16, HD), bf16),
            vm((HEADS * ROWS, HD), f32),
            vm((ROWS, HEADS, HD), f32),
            vm((ROWS, HD), f32),
            vm((ROWS, HD), f32),
            vm((4, HEADS, BLOCK), f32),
            vm((4, HEADS, BLOCK), bf16),
            vm((2, KVH, 48, HD), bf16),
            vm((17, 48, HD), bf16),
            vm((48, HD), bf16),
            vm((NWIDE, 48, HD), bf16),
            vm((HEADS, HD), f32),
            vm((ROWS, WIDTH), f32),
            vm((NSEQ, ROWS, WIDTH), f32),
            pltpu.SemaphoreType.DMA((9,)),
            pltpu.SemaphoreType.DMA((ROWS,)),
            pltpu.SemaphoreType.DMA((ROWS,)),
            pltpu.SemaphoreType.DMA((8,)),
            pltpu.SemaphoreType.DMA((8,)),
        ],
        compiler_params=pltpu.CompilerParams(
            collective_id=0, has_side_effects=True, vmem_limit_bytes=60 * 1024 * 1024
        ),
    )(
        activations,
        attn_gain,
        w_query,
        w_keyval.reshape(2 * WIDTH, HD),
        w_output.T,
        query_gain.reshape(1, HD),
        key_gain.reshape(1, HD),
        key_cache.reshape(ROWS, FLAT, HD),
        value_cache.reshape(ROWS, FLAT, HD),
        freq,
        lengths,
    )


def solution(mesh):
    return jax.shard_map(
        body,
        mesh=mesh,
        in_specs=(
            P(None, "wide"),
            P("wide"),
            P("wide", "seq"),
            P("wide", None, "seq"),
            P("seq", "wide"),
            P(),
            P(),
            P(None, ("seq", "wide"), None, None),
            P(None, ("seq", "wide"), None, None),
            P(),
        ),
        out_specs=P(None, "wide"),
        check_vma=False,
    )
```

```python
import math

import jax
import jax.numpy as jnp
import numpy as np
from jax import lax
from jax.experimental import pallas as pl
from jax.experimental.pallas import tpu as pltpu
from jax.sharding import PartitionSpec as P

rope_base = 1000000.0
eps_norm = 1e-06
neg_large = -1e30
MESH = pl.DeviceIdType.MESH
f32 = jnp.float32
bf16 = jnp.bfloat16

ROWS, KVH, GROUP, HD = 8, 8, 8, 128
HEADS = KVH * GROUP
BLOCK = 512
FLAT = BLOCK * KVH
NSEQ, NWIDE = 8, 16
WIDTH = 320
D = 5120


def lane_iota(shape):
    return lax.broadcasted_iota(jnp.int32, shape, len(shape) - 1)


def kernel(
    x_hbm, gain_hbm, wq_hbm, wkv_hbm, wo_hbm, qg_hbm, kg_hbm, k_hbm, v_hbm, freq_hbm, len_hbm,
    out_ref,
    x_v, gain_v, wq_v, wkv_v, wo_v, qg_v, kg_v, k_v, v_v, freq_v,
    len_ref, k_t, v_r, s1, r1, skv, rkv, sq, qall, qf, qt, knew, vnew, scr, pb,
    s3, r3, s4, r4, of, s5, r5,
    in_sem, k_sem, v_sem, ssem, rsem,
):
    s = lax.axis_index("seq")
    w = lax.axis_index("wide")
    x = w // 4
    yh = (w // 2) % 2
    core = w % 2
    yl = s // 4
    z = s % 4

    small = [
        pltpu.make_async_copy(a, b, in_sem.at[i])
        for i, (a, b) in enumerate(
            [
                (x_hbm, x_v),
                (gain_hbm, gain_v),
                (wq_hbm, wq_v),
                (qg_hbm, qg_v),
                (kg_hbm, kg_v),
                (freq_hbm, freq_v),
                (wkv_hbm, wkv_v),
                (wo_hbm, wo_v),
                (len_hbm, len_ref),
            ]
        )
    ]

    def ring(k):
        return min(k, 4 - k)

    def y_hops(hi, lo):
        return 1 if lo else 2 * hi

    steps = [(kx, hi, kc) for kx in range(4) for hi in range(2) for kc in range(2)]
    steps.sort(key=lambda k: (-ring(k[0]) - y_hops(k[1], 0), -k[2]))
    wide_to = [
        ((x + kx) % 4) * 4 + ((yh + hi) % 2) * 2 + (core + kc) % 2
        for kx, hi, kc in steps
        if kx or hi or kc
    ]
    steps = [
        (kz, hi, lo, kc)
        for kz in range(4)
        for hi in range(2)
        for lo in range(2)
        for kc in range(2)
    ]
    steps.sort(key=lambda k: (-ring(k[0]) - y_hops(k[1], k[2]), -k[3]))
    plane_to = [
        (
            ((yl + lo) % 2) * 4 + (z + kz) % 4,
            x * 4 + ((yh + hi) % 2) * 2 + (core + kc) % 2,
            bool(kz or lo),
        )
        for kz, hi, lo, kc in steps
        if kz or hi or lo or kc
    ]
    steps = [(kz, lo) for kz in range(4) for lo in range(2)]
    steps.sort(key=lambda k: -ring(k[0]) - k[1])
    seq_to = [((yl + lo) % 2) * 4 + (z + kz) % 4 for kz, lo in steps if kz or lo]

    for c in small[:3]:
        c.start()
    bar = pltpu.get_barrier_semaphore()
    n_bar = 0
    for tw in wide_to:
        pl.semaphore_signal(bar, inc=1, device_id=(s, tw), device_id_type=MESH)
        n_bar += 1
    for ts, tw, far in plane_to:
        if far:
            pl.semaphore_signal(bar, inc=1, device_id=(ts, tw), device_id_type=MESH)
            n_bar += 1

    def remote(src, dst, i, to):
        return pltpu.make_async_remote_copy(
            src_ref=src, dst_ref=dst, send_sem=ssem.at[i], recv_sem=rsem.at[i],
            device_id=to, device_id_type=MESH,
        )

    for c in small[3:]:
        c.start()
    k_cp = [pltpu.make_async_copy(k_hbm.at[b], k_v.at[b], k_sem.at[b]) for b in range(ROWS)]
    v_cp = [pltpu.make_async_copy(v_hbm.at[b], v_v.at[b], v_sem.at[b]) for b in range(ROWS)]
    for c in k_cp + v_cp:
        c.start()

    for c in small[:3]:
        c.wait()
    xf = x_v[...].astype(f32)
    ss = jnp.sum(xf * xf, axis=-1, keepdims=True)
    normed = (xf * gain_v[...][None, :]).astype(bf16)
    row = lax.broadcasted_iota(jnp.int32, (ROWS, HD), 0)
    lane = lane_iota((ROWS, HD))
    ss_row = jnp.sum(jnp.where(lane == row, ss, 0.0), axis=0, keepdims=True)
    for p in range(4):
        part = jnp.dot(normed, wq_v[:, p * 256 : (p + 1) * 256], preferred_element_type=f32)
        s1[p, 0:ROWS] = part[:, :HD]
        s1[p, ROWS : 2 * ROWS] = part[:, HD:]
        s1[p, 2 * ROWS : 2 * ROWS + 1] = ss_row
    r1[w] = s1[w % 4]

    def turn_k(b, carry):
        pltpu.make_async_copy(k_hbm.at[b], k_v.at[b], k_sem.at[b]).wait()
        for ch in range(2):
            part = k_v[b, pl.ds(ch * 2048, 2048), :].reshape(256, KVH, HD).reshape(256, KVH * HD)
            k_t[b, :, ch * 256 : (ch + 1) * 256] = part.T
        return carry

    def turn_v(b, carry):
        pltpu.make_async_copy(v_hbm.at[b], v_v.at[b], v_sem.at[b]).wait()
        for ch in range(2):
            part = v_v[b, pl.ds(ch * 2048, 2048), :].reshape(256, KVH, HD)
            v_r[b, pl.ds(ch * 256, 256), :] = part.reshape(256, KVH * HD)
        return carry

    pl.semaphore_wait(bar, n_bar)
    for tw in wide_to:
        remote(s1.at[tw % 4], r1.at[w], 0, (s, tw)).start()

    for c in small[3:7]:
        c.wait()
    row_i = lax.broadcasted_iota(jnp.int32, (WIDTH, 2 * WIDTH), 0)
    col_i = lax.broadcasted_iota(jnp.int32, (WIDTH, 2 * WIDTH), 1)
    spread = jnp.where(col_i // 2 == row_i, 1.0, 0.0).astype(bf16)
    twice = jnp.dot(normed, spread, preferred_element_type=f32)
    odd = lane_iota((ROWS, 2 * WIDTH)) % 2
    both = jnp.concatenate(
        [jnp.where(odd == 0, twice, 0.0), jnp.where(odd == 1, twice, 0.0)], axis=0
    ).astype(bf16)
    kv_part = jnp.dot(both, wkv_v[...], preferred_element_type=f32)
    skv[0] = kv_part[:ROWS]
    skv[1] = kv_part[ROWS:]

    small[8].wait()
    lens = jnp.zeros((ROWS, HD), jnp.int32)
    for b in range(ROWS):
        lens = jnp.where(row == b, len_ref[b], lens)
    angle = lens.astype(f32) * freq_v[...]
    cosine = jnp.cos(angle)
    sine = jnp.where(lane < HD // 2, -jnp.sin(angle), jnp.sin(angle))

    def head(u, inv_rms, gain):
        mean = jnp.mean(u * u, axis=-1, keepdims=True) * (inv_rms * inv_rms)
        u = u * gain * (inv_rms * lax.rsqrt(mean + eps_norm))
        return u * cosine + pltpu.roll(u, HD // 2, 1) * sine

    for t in range(2):

        @pl.when(w != t)
        def _():
            remote(skv, rkv.at[w], 1, (s, t)).start()

        @pl.when(w == t)
        def _():
            rkv[w] = skv[...]

    lax.fori_loop(0, 4, turn_k, 0)

    remote(r1.at[pl.ds(0, NWIDE - 1)], r1.at[pl.ds(0, NWIDE - 1)], 0, (s, w)).wait_recv()
    tot = r1[0]
    for i in range(1, NWIDE):
        tot = tot + r1[i]
    ss = jnp.sum(
        jnp.where(lane == row, tot[2 * ROWS : 2 * ROWS + 1], 0.0), axis=-1, keepdims=True
    )
    inv_rms = lax.rsqrt(ss / D + eps_norm)
    sq[...] = jnp.concatenate(
        [head(tot[:ROWS], inv_rms, qg_v[...]), head(tot[ROWS : 2 * ROWS], inv_rms, qg_v[...])],
        axis=0,
    ).astype(bf16)

    p_own = w % 4
    for ts, tw, _far in plane_to:
        remote(sq, qall.at[s * 4 + p_own], 2, (ts, tw)).start()
    qall[s * 4 + p_own] = sq[...]

    lax.fori_loop(4, ROWS, turn_k, 0)
    lax.fori_loop(0, ROWS, turn_v, 0)

    remote(qall.at[pl.ds(0, 31)], qall.at[pl.ds(0, 31)], 2, (s, w)).wait_recv()
    qf[...] = qall[...].reshape(HEADS * ROWS, HD).astype(f32)
    for b in range(ROWS):
        qt[b] = qf[pl.ds(b, HEADS, stride=ROWS), :]

    scale = HD ** (-0.5)
    start = (s * NWIDE + w) * BLOCK
    plane = lane_iota((HEADS, BLOCK))
    none = jnp.zeros((GROUP, HD), f32)
    block32 = lane_iota((HEADS, HD)) // 32
    low = lane_iota((HEADS, HD)) % 32 < 16
    low16 = lane % 32 < 16

    def by_block(parts):
        n = parts[0].shape[0]
        out = parts[0]
        for i in range(1, 4):
            out = jnp.where(block32[:n] == i, parts[i], out)
        return out

    def pack(peak, total):
        high = total.astype(bf16).astype(f32)
        n = low[: peak.shape[0]]
        return jnp.where(n, peak, high), jnp.where(n, 0.0, total - high)

    slot3 = s * 2 + core
    def half(c, carry):
        c = (core + c) % 2
        rows = [c * 4 + i for i in range(4)]
        scores, peaks, totals, weights, numers = {}, {}, {}, {}, {}
        for i, b in enumerate(rows):
            parts = []
            for pr in range(4):
                one = qt[b, 16 * pr : 16 * pr + 8, :]
                two = qt[b, 16 * pr + 8 : 16 * pr + 16, :]
                lhs = jnp.concatenate(
                    [jnp.concatenate([one, none], axis=1), jnp.concatenate([none, two], axis=1)],
                    axis=0,
                ).astype(bf16)
                keys = k_t[b, pr * 256 : (pr + 1) * 256, :]
                parts.append(jnp.dot(lhs, keys, preferred_element_type=f32))
            scr[i] = jnp.concatenate(parts, axis=0)
        for i, b in enumerate(rows):
            valid = plane < len_ref[b] - start
            t = jnp.where(valid, scr[i] * scale, neg_large)
            m = jnp.max(t, axis=-1, keepdims=True).astype(bf16).astype(f32)
            e = jnp.where(valid, jnp.exp(t - m), 0.0)
            peaks[i] = jnp.broadcast_to(m, (HEADS, HD))
            totals[i] = jnp.broadcast_to(jnp.sum(e, axis=-1, keepdims=True), (HEADS, HD))
            pb[i] = e.astype(bf16)
        for i, b in enumerate(rows):
            for pr in range(4):
                n = jnp.dot(
                    pb[i, 16 * pr : 16 * pr + 16, :],
                    v_r[b, :, pr * 256 : (pr + 1) * 256],
                    preferred_element_type=f32,
                )
                numers[i, 2 * pr] = n[:GROUP, :HD]
                numers[i, 2 * pr + 1] = n[GROUP:, HD:]
        stats = pack(by_block([peaks[i] for i in range(4)]), by_block([totals[i] for i in range(4)]))
        for g in range(KVH):
            own = slice(g * GROUP, (g + 1) * GROUP)
            s3[c, g] = jnp.concatenate(
                [numers[i, g] for i in range(4)] + [part[own] for part in stats], axis=0
            ).astype(bf16)
        tw = w - core + c
        for ts in seq_to:
            remote(s3.at[c, ts], r3.at[slot3], 3, (ts, tw)).start()

        @pl.when(core != c)
        def _():
            remote(s3.at[c, s], r3.at[slot3], 3, (s, tw)).start()

        @pl.when(core == c)
        def _():
            r3[slot3] = s3[c, s]
        return carry

    half(0, 0)
    half(1, 0)

    @pl.when(w < 2)
    def _():
        remote(rkv.at[pl.ds(0, NWIDE - 1)], rkv.at[pl.ds(0, NWIDE - 1)], 1, (s, w)).wait_recv()
        kv = rkv[0]
        for i in range(1, NWIDE):
            kv = kv + rkv[i]
        knew[...] = head(kv[0], inv_rms, kg_v[...]).astype(bf16).astype(f32)
        vnew[...] = (kv[1] * inv_rms).astype(bf16).astype(f32)

    @pl.when(w < 2)
    def _():
        peaks, totals, numers = [], [], []
        for i in range(4):
            b = core * 4 + i
            qrow = qt[b, pl.ds(s * GROUP, GROUP), :]
            sn = jnp.sum(qrow * knew[pl.ds(b, 1), :], axis=-1, keepdims=True) * scale
            sn = jnp.broadcast_to(sn, (GROUP, HD))
            mn = sn.astype(bf16).astype(f32)
            pn = jnp.exp(sn - mn)
            peaks.append(mn)
            totals.append(pn)
            numers.append(pn.astype(bf16).astype(f32) * vnew[pl.ds(b, 1), :])
        r3[16] = jnp.concatenate(
            numers + list(pack(by_block(peaks), by_block(totals))), axis=0
        ).astype(bf16)

    @pl.when(w >= 2)
    def _():
        r3[16] = jnp.concatenate(
            [jnp.zeros((32, HD), f32)]
            + list(pack(jnp.full((GROUP, HD), neg_large, f32), jnp.zeros((GROUP, HD), f32))),
            axis=0,
        ).astype(bf16)

    remote(r3.at[pl.ds(0, 15)], r3.at[pl.ds(0, 15)], 3, (s, w)).wait_recv()

    def merge(messages):
        messages = [msg.astype(f32) for msg in messages]
        high = [msg[32:40] for msg in messages]
        peak = high[0]
        for t in high[1:]:
            peak = jnp.maximum(peak, t)
        total = jnp.zeros((GROUP, HD), f32)
        acc = [jnp.zeros((GROUP, HD), f32) for _ in range(4)]
        for t, msg in zip(high, messages):
            f = jnp.exp(t - peak)
            total = total + f * pltpu.roll(t + msg[40:48], HD - 16, 1)
            for i in range(4):
                acc[i] = acc[i] + jnp.broadcast_to(f[:, 32 * i : 32 * i + 1], (GROUP, HD)) * msg[
                    i * GROUP : (i + 1) * GROUP
                ]
        return peak, total, acc

    peak, total, acc = merge([r3[i] for i in range(17)])
    s4[...] = jnp.concatenate(acc + list(pack(peak, pltpu.roll(total, 16, 1))), axis=0).astype(bf16)
    for tw in wide_to:
        remote(s4, r4.at[w], 5, (s, tw)).start()
    r4[w] = s4[...]
    small[7].wait()
    remote(r4.at[pl.ds(0, 15)], r4.at[pl.ds(0, 15)], 5, (s, w)).wait_recv()
    for c in range(2):
        peak, total, acc = merge([r4[2 * i + c] for i in range(8)])
        for i in range(4):
            den = jnp.broadcast_to(total[:, 32 * i : 32 * i + 1], (GROUP, HD))
            of[pl.ds((c * 4 + i) * GROUP, GROUP), :] = acc[i] / den

    o = jnp.concatenate(
        [of[pl.ds(j, ROWS, stride=GROUP), :].astype(bf16) for j in range(GROUP)], axis=1
    )
    s5[...] = lax.dot_general(o, wo_v[...], (((1,), (1,)), ((), ())), preferred_element_type=f32)
    for ts in seq_to:
        remote(s5, r5.at[s], 7, (ts, w)).start()
    r5[s] = s5[...]
    remote(r5.at[pl.ds(0, 7)], r5.at[pl.ds(0, 7)], 7, (s, w)).wait_recv()
    out = r5[0]
    for i in range(1, NSEQ):
        out = out + r5[i]
    out_ref[...] = out

    remote(r1.at[pl.ds(0, 15)], r1.at[pl.ds(0, 15)], 0, (s, w)).wait_send()
    for t in range(2):

        @pl.when(w != t)
        def _():
            remote(skv, rkv.at[w], 1, (s, t)).wait_send()

    remote(qall.at[pl.ds(0, 31)], qall.at[pl.ds(0, 31)], 2, (s, w)).wait_send()
    remote(r3.at[pl.ds(0, 15)], r3.at[pl.ds(0, 15)], 3, (s, w)).wait_send()
    remote(r4.at[pl.ds(0, 15)], r4.at[pl.ds(0, 15)], 5, (s, w)).wait_send()
    remote(r5.at[pl.ds(0, 7)], r5.at[pl.ds(0, 7)], 7, (s, w)).wait_send()


def body(
    activations, attn_gain, w_query, w_keyval, w_output, query_gain, key_gain, key_cache, value_cache, lengths
):
    half = HD // 2
    freq = np.exp(-(2.0 * np.arange(half) / HD) * math.log(rope_base)).astype(np.float32)
    freq = jnp.asarray(np.concatenate([freq, freq])[None, :])
    any_spec = pl.BlockSpec(memory_space=pl.ANY)
    vm = pltpu.VMEM
    return pl.pallas_call(
        kernel,
        out_shape=pltpu.VMEM((ROWS, WIDTH), f32),
        in_specs=[any_spec] * 11,
        out_specs=pl.BlockSpec(memory_space=pltpu.VMEM),
        scratch_shapes=[
            vm((ROWS, WIDTH), bf16),
            vm((WIDTH,), f32),
            vm((WIDTH, 1024), bf16),
            vm((2 * WIDTH, HD), bf16),
            vm((WIDTH, 1024), bf16),
            vm((1, HD), f32),
            vm((1, HD), f32),
            vm((ROWS, FLAT, HD), bf16),
            vm((ROWS, FLAT, HD), bf16),
            vm((1, HD), f32),
            pltpu.SMEM((ROWS,), jnp.int32),
            vm((ROWS, KVH * HD, BLOCK), bf16),
            vm((ROWS, BLOCK, KVH * HD), bf16),
            vm((4, 17, HD), f32),
            vm((NWIDE, 17, HD), f32),
            vm((2, ROWS, HD), f32),
            vm((NWIDE, 2, ROWS, HD), f32),
            vm((16, HD), bf16),
            vm((32, 16, HD), bf16),
            vm((HEADS * ROWS, HD), f32),
            vm((ROWS, HEADS, HD), f32),
            vm((ROWS, HD), f32),
            vm((ROWS, HD), f32),
            vm((4, HEADS, BLOCK), f32),
            vm((4, HEADS, BLOCK), bf16),
            vm((2, KVH, 48, HD), bf16),
            vm((17, 48, HD), bf16),
            vm((48, HD), bf16),
            vm((NWIDE, 48, HD), bf16),
            vm((HEADS, HD), f32),
            vm((ROWS, WIDTH), f32),
            vm((NSEQ, ROWS, WIDTH), f32),
            pltpu.SemaphoreType.DMA((9,)),
            pltpu.SemaphoreType.DMA((ROWS,)),
            pltpu.SemaphoreType.DMA((ROWS,)),
            pltpu.SemaphoreType.DMA((8,)),
            pltpu.SemaphoreType.DMA((8,)),
        ],
        compiler_params=pltpu.CompilerParams(
            collective_id=0, has_side_effects=True, vmem_limit_bytes=60 * 1024 * 1024
        ),
    )(
        activations,
        attn_gain,
        w_query,
        w_keyval.reshape(2 * WIDTH, HD),
        w_output.T,
        query_gain.reshape(1, HD),
        key_gain.reshape(1, HD),
        key_cache.reshape(ROWS, FLAT, HD),
        value_cache.reshape(ROWS, FLAT, HD),
        freq,
        lengths,
    )


def solution(mesh):
    return jax.shard_map(
        body,
        mesh=mesh,
        in_specs=(
            P(None, "wide"),
            P("wide"),
            P("wide", "seq"),
            P("wide", None, "seq"),
            P("seq", "wide"),
            P(),
            P(),
            P(None, ("seq", "wide"), None, None),
            P(None, ("seq", "wide"), None, None),
            P(),
        ),
        out_specs=P(None, "wide"),
        check_vma=False,
    )
```
